32 devices in a mesh: dp: 16 (over z, y, core), gz: 2 (over x).
Axes of the slice: x: 2, y: 2, z: 4, core: 2. Of those that a mesh axis runs over, the one named last changes fastest.
Arguments:
- features_in: bfloat16 [16, 32, 8, 512], P('dp', None, 'gz'), may hold values from -6 to 6
- kernel_taps: bfloat16 [27, 2048], replicated, may hold values from -0.21875 to 0.21875
- channel_bias: float32 [64], replicated, may hold values from -3 to 3
- upstream: bfloat16 [16, 64, 8, 512], P('dp', None, 'gz'), may hold values from -6 to 6
Outputs:
- output: bfloat16 [16, 64, 8, 512], P('dp', None, 'gz')
- grad_input: bfloat16 [16, 32, 8, 512], P('dp', None, 'gz')
- weight_grad: float32 [27, 2048], replicated
- bias_grad: float32 [64], replicated
The draws below stay inside these ranges and needn't reach their ends.
All inputs are finite; a program needn't handle non-finite values.
Results may differ from the reference program's by a relative error of at most 0.0034.
Values may be sent and summed in bfloat16 or wider, within the bound.
A program may use at most 64 MiB of HBM per device.

```python
import math
import jax
import jax.numpy as jnp
from jax import lax

CIN = 32
COUT = 64
NX = 64
NY = 8
VOLUMES = 16
NZ = 8


def shard_levels(stream_key, extent, shards, low, high):
    level, own = 1.0, jax.random.fold_in(stream_key, 6)
    for axis_at, blocks in shards:
        draws = jnp.exp(jax.random.uniform(jax.random.fold_in(own, axis_at), (blocks,), jnp.float32, low / len(shards), high / len(shards)))
        level = level * jnp.repeat(draws, extent[axis_at] // blocks).reshape([-1 if axis == axis_at else 1 for axis in range(len(extent))])
    return level


def centred(key, shape, spread, bound, pieces=(), kind=jnp.bfloat16):
    array = jax.random.normal(key, shape, jnp.float32) * spread
    if len(pieces) > 0:
        array = shard_levels(key, shape, pieces, -0.22, 0.18) * array
    return jnp.clip(array, min=-bound, max=bound).astype(kind)


def setup_inputs(seed: int = 0) -> dict:
    arg_keys = jax.random.split(jax.random.key(seed), 5)
    features_in = centred(arg_keys[0], (VOLUMES, CIN, NZ, NY * NX), 1.0, 6.0, ((0, 16), (2, 2)))
    kernel_taps = centred(arg_keys[1], (27, CIN * COUT), (27 * CIN) ** -0.5, 0.21875)
    channel_bias = centred(arg_keys[2], (COUT,), 0.5, 3.0, (), jnp.float32)
    upstream = centred(arg_keys[3], (VOLUMES, COUT, NZ, NY * NX), 1.0, 6.0, ((0, 16), (2, 2)))
    return {"features_in": features_in, "kernel_taps": kernel_taps, "channel_bias": channel_bias, "upstream": upstream}


def correlate(field, taps):
    return lax.conv_general_dilated(field, taps, (1, 1, 1), 'VALID', dimension_numbers=('NCDHW', 'DHWIO', 'NCDHW'), precision=lax.Precision.HIGHEST)

def reference(features_in, kernel_taps, channel_bias, upstream):
    kernel = kernel_taps.astype(jnp.float32).reshape(3, 3, 3, CIN, COUT)
    flipped = jnp.transpose(kernel[::-1, ::-1, ::-1], (0, 1, 2, 4, 3))
    widths = ((0, 0), (0, 0), (1, 1), (1, 1), (1, 1))
    feats = features_in.reshape(VOLUMES, CIN, NZ, NY, NX)
    grads = upstream.reshape(VOLUMES, COUT, NZ, NY, NX)

    def one_volume(carry, pair):
        field, grad = pair
        padded_in = jnp.pad(field.astype(jnp.float32)[None], widths)
        grad_whole = grad.astype(jnp.float32)[None]
        padded_up = jnp.pad(grad_whole, widths)
        result = correlate(padded_in, kernel) + channel_bias.astype(jnp.float32)[None, :, None, None, None]
        back = correlate(padded_up, flipped)
        weight_term = lax.conv_general_dilated(padded_in, grad_whole, (1, 1, 1), 'VALID', dimension_numbers=('CNDHW', 'IODHW', 'DHWNC'), precision=lax.Precision.HIGHEST)
        weight_term = weight_term.reshape(27, CIN * COUT)
        bias_term = lax.optimization_barrier(jnp.sum(grad_whole, axis=(0, 2, 3, 4)))
        return ((carry[0] + weight_term, carry[1] + bias_term), (result[0].astype(jnp.bfloat16), back[0].astype(jnp.bfloat16)))
    start = (jnp.zeros((27, CIN * COUT), jnp.float32), jnp.zeros((COUT,), jnp.float32))
    totals, results = lax.scan(one_volume, start, (feats, grads))
    factor = 1.0 / math.sqrt(VOLUMES * NZ * NY * NX)
    out_main = results[0].reshape(VOLUMES, COUT, NZ, NY * NX)
    out_back = results[1].reshape(VOLUMES, CIN, NZ, NY * NX)
    return (out_main, out_back, totals[0] * factor, totals[1] * factor)
```

```python
import functools
import math

import jax
import jax.numpy as jnp
from jax import lax
from jax.experimental import pallas as pl
from jax.experimental.pallas import tpu as pltpu
from jax.sharding import PartitionSpec as P

NX = 64
NY = 8
MESH = pl.DeviceIdType.MESH
LANES = 128
ROWS = 16


def shifted(plane):
    cells = plane.shape[1]
    field = plane.astype(jnp.float32)
    at = lax.broadcasted_iota(jnp.int32, (1, cells), 1)
    col = at % NX
    zero = jnp.zeros_like(field)
    sides = (
        jnp.where(col == 0, zero, pltpu.roll(field, 1, 1)),
        field,
        jnp.where(col == NX - 1, zero, pltpu.roll(field, cells - 1, 1)),
    )
    found = [jnp.where(at < NX, zero, pltpu.roll(side, NX, 1)) for side in sides]
    found += list(sides)
    found += [jnp.where(at >= cells - NX, zero, pltpu.roll(side, cells - NX, 1)) for side in sides]
    return [each.astype(jnp.bfloat16) for each in found]


def fill(buf, vol, slot, plane):
    chan = plane.shape[0]
    for tap, value in enumerate(shifted(plane)):
        buf[vol, pl.ds((slot * 9 + tap) * chan, chan), :] = value


def kernel(
    sizes, factor, x_ref, u_ref, wf_ref, wb_ref, bias_ref, out_ref, gi_ref, wg_ref,
    halo_x, halo_u, near_x, near_u, part, recv_in, acc, recv_out, gath,
    halo_send, halo_recv, in_send, in_recv, out_send, out_recv,
    gout_send, gout_recv, gin_send, gin_recv,
):
    inner_dp, n_gz, n_in, n_out = sizes
    vols, planes, in_chan, cells = x_ref.shape
    out_chan = u_ref.shape[2]
    dp, gz = lax.axis_index("dp"), lax.axis_index("gz")
    me_in = lax.rem(dp, inner_dp) * n_gz + gz
    me_out = lax.div(dp, inner_dp)

    def inner_peer(step):
        peer = lax.rem(me_in + step, n_in)
        return peer, {"dp": me_out * inner_dp + lax.div(peer, n_gz), "gz": lax.rem(peer, n_gz)}

    def outer_peer(step):
        peer = lax.rem(me_out + step, n_out)
        return peer, {"dp": peer * inner_dp + lax.rem(dp, inner_dp), "gz": gz}

    barrier = pltpu.get_barrier_semaphore()
    for step in range(1, n_in):
        pl.semaphore_signal(barrier, inc=1, device_id=inner_peer(step)[1], device_id_type=MESH)
    for step in range(1, n_out):
        pl.semaphore_signal(barrier, inc=1, device_id=outer_peer(step)[1], device_id_type=MESH)
    pl.semaphore_wait(barrier, n_in + n_out - 2)

    def halo_copies(side):
        source = planes - 1 if side == 0 else 0
        target = gz + 1 if side == 0 else gz - 1
        return [
            pltpu.make_async_remote_copy(
                src_ref=ref.at[:, source],
                dst_ref=halo.at[side],
                send_sem=halo_send.at[side, at],
                recv_sem=halo_recv.at[side, at],
                device_id={"gz": target},
                device_id_type=MESH,
            )
            for at, (ref, halo) in enumerate(((x_ref, halo_x), (u_ref, halo_u)))
        ]

    sends = (gz < n_gz - 1, gz > 0)
    gets = (gz > 0, gz < n_gz - 1)
    for side in range(2):

        @pl.when(sends[side])
        def _(side=side):
            for copy in halo_copies(side):
                copy.start()

    for vol in range(vols):
        for z in range(planes):
            fill(near_x, vol, z + 1, x_ref[vol, z])
            fill(near_u, vol, z + 1, u_ref[vol, z])

    for side in range(2):

        @pl.when(gets[side])
        def _(side=side):
            for copy in halo_copies(side):
                copy.wait_recv()

        @pl.when(jnp.logical_not(gets[side]))
        def _(side=side):
            halo_x[side] = jnp.zeros(halo_x.shape[1:], halo_x.dtype)
            halo_u[side] = jnp.zeros(halo_u.shape[1:], halo_u.dtype)

    for vol in range(vols):
        for side, slot in ((0, 0), (1, planes + 1)):
            fill(near_x, vol, slot, halo_x[side, vol])

    deep_x, deep_u = 9 * in_chan, 9 * out_chan
    term = jnp.zeros((3 * deep_x, out_chan), jnp.float32)
    bias_term = jnp.zeros((8, out_chan), jnp.float32)
    ones = jnp.ones((8, cells), jnp.bfloat16)
    lanes = (((1,), (1,)), ((), ()))
    for vol in range(vols):
        for z in range(planes):
            grad = u_ref[vol, z]
            window = near_x[vol, pl.ds(z * deep_x, 3 * deep_x), :]
            term += lax.dot_general(window, grad, lanes, preferred_element_type=jnp.float32)
            bias_term += lax.dot_general(ones, grad, lanes, preferred_element_type=jnp.float32)
    half = in_chan // 2
    term = term.reshape(27, 2, half, out_chan)
    term = jnp.concatenate([term[:, 0], term[:, 1]], axis=-1).reshape(27 * half, 2 * out_chan)
    bias_term = jnp.concatenate([bias_term, jnp.zeros_like(bias_term)], axis=-1)
    chunk = part.shape[1]
    filled = 27 * half + 8
    whole = jnp.concatenate(
        [term, bias_term, jnp.zeros((n_in * chunk - filled, LANES), jnp.float32)], axis=0
    )
    part[...] = whole.reshape(part.shape)

    def in_copy(step):
        peer, device = inner_peer(step)
        return pltpu.make_async_remote_copy(
            src_ref=part.at[peer],
            dst_ref=recv_in.at[step - 1],
            send_sem=in_send.at[step - 1],
            recv_sem=in_recv.at[step - 1],
            device_id=device,
            device_id_type=MESH,
        )

    def out_copy(step):
        peer, device = outer_peer(step)
        return pltpu.make_async_remote_copy(
            src_ref=acc.at[peer],
            dst_ref=recv_out.at[step - 1],
            send_sem=out_send.at[step - 1],
            recv_sem=out_recv.at[step - 1],
            device_id=device,
            device_id_type=MESH,
        )

    def gather_out_copy(step):
        return pltpu.make_async_remote_copy(
            src_ref=gath.at[me_in, me_out],
            dst_ref=gath.at[me_in, me_out],
            send_sem=gout_send.at[step - 1],
            recv_sem=gout_recv.at[step - 1],
            device_id=outer_peer(step)[1],
            device_id_type=MESH,
        )

    def gather_in_copy(step):
        return pltpu.make_async_remote_copy(
            src_ref=gath.at[me_in],
            dst_ref=gath.at[me_in],
            send_sem=gin_send.at[step - 1],
            recv_sem=gin_recv.at[step - 1],
            device_id=inner_peer(step)[1],
            device_id_type=MESH,
        )

    for step in range(1, n_in):
        in_copy(step).start()

    rows = (((1,), (0,)), ((), ()))
    for vol in range(vols):
        for z in range(planes):
            window = near_x[vol, pl.ds(z * deep_x, 3 * deep_x), :]
            value = lax.dot_general(wf_ref[...], window, rows, preferred_element_type=jnp.float32)
            out_ref[vol, z] = (value + bias_ref[...]).astype(jnp.bfloat16)

    for step in range(1, n_in):
        in_copy(step).wait_recv()
    total = part[me_in]
    for step in range(1, n_in):
        total += recv_in[step - 1]
    acc[...] = total.reshape(acc.shape)
    for step in range(1, n_out):
        out_copy(step).start()

    for vol in range(vols):
        for side, slot in ((0, 0), (1, planes + 1)):
            fill(near_u, vol, slot, halo_u[side, vol])
    for vol in range(vols):
        for z in range(planes):
            window = near_u[vol, pl.ds(z * deep_u, 3 * deep_u), :]
            value = lax.dot_general(wb_ref[...], window, rows, preferred_element_type=jnp.float32)
            gi_ref[vol, z] = value.astype(jnp.bfloat16)

    for step in range(1, n_out):
        out_copy(step).wait_recv()
    total = acc[me_out]
    for step in range(1, n_out):
        total += recv_out[step - 1]
    gath[me_in, me_out] = (total * factor).astype(jnp.bfloat16)
    for step in range(1, n_out):
        gather_out_copy(step).start()
    for step in range(1, n_out):
        gather_out_copy(step).wait_recv()
    for step in range(1, n_in):
        gather_in_copy(step).start()
    for step in range(1, n_in):
        gather_in_copy(step).wait_recv()
    wg_ref[...] = gath[...].reshape(wg_ref.shape)

    for side in range(2):

        @pl.when(sends[side])
        def _(side=side):
            for copy in halo_copies(side):
                copy.wait_send()

    for step in range(1, n_in):
        in_copy(step).wait_send()
        gather_in_copy(step).wait_send()
    for step in range(1, n_out):
        out_copy(step).wait_send()
        gather_out_copy(step).wait_send()


def on_device(sizes, features_in, kernel_taps, channel_bias, upstream):
    inner_dp, n_gz, n_in, n_out = sizes
    vols, in_chan, planes, cells = features_in.shape
    out_chan = upstream.shape[1]
    half = in_chan // 2
    x = features_in.reshape(vols, half, 2, planes, cells).transpose(0, 3, 2, 1, 4)
    x = x.reshape(vols, planes, in_chan, cells)
    u = upstream.transpose(0, 2, 1, 3)
    taps = kernel_taps.reshape(27, half, 2, out_chan)
    wf = taps.transpose(3, 0, 2, 1).reshape(out_chan, 27 * in_chan)
    wb = kernel_taps.reshape(27, in_chan, out_chan)[::-1].transpose(1, 0, 2)
    wb = wb.reshape(in_chan, 27 * out_chan)
    cells_all = vols * inner_dp * n_out * planes * n_gz * cells
    factor = 1.0 / math.sqrt(cells_all)
    filled = 27 * half + 8
    per = ROWS * -(-filled // (ROWS * n_in * n_out))
    vmem = pl.BlockSpec(memory_space=pltpu.VMEM)
    dma = pltpu.SemaphoreType.DMA
    steps_in, steps_out = max(n_in - 1, 1), max(n_out - 1, 1)
    out, gi, wg = pl.pallas_call(
        functools.partial(kernel, sizes, factor),
        out_shape=(
            jax.ShapeDtypeStruct((vols, planes, out_chan, cells), jnp.bfloat16),
            jax.ShapeDtypeStruct((vols, planes, in_chan, cells), jnp.bfloat16),
            jax.ShapeDtypeStruct((n_in * n_out * per, LANES), jnp.bfloat16),
        ),
        in_specs=[vmem] * 5,
        out_specs=(vmem,) * 3,
        scratch_shapes=[
            pltpu.VMEM((2, vols, in_chan, cells), jnp.bfloat16),
            pltpu.VMEM((2, vols, out_chan, cells), jnp.bfloat16),
            pltpu.VMEM((vols, (planes + 2) * 9 * in_chan, cells), jnp.bfloat16),
            pltpu.VMEM((vols, (planes + 2) * 9 * out_chan, cells), jnp.bfloat16),
            pltpu.VMEM((n_in, n_out * per, LANES), jnp.float32),
            pltpu.VMEM((steps_in, n_out * per, LANES), jnp.float32),
            pltpu.VMEM((n_out, per, LANES), jnp.float32),
            pltpu.VMEM((steps_out, per, LANES), jnp.float32),
            pltpu.VMEM((n_in, n_out, per, LANES), jnp.bfloat16),
            dma((2, 2)),
            dma((2, 2)),
            dma((steps_in,)),
            dma((steps_in,)),
            dma((steps_out,)),
            dma((steps_out,)),
            dma((steps_out,)),
            dma((steps_out,)),
            dma((steps_in,)),
            dma((steps_in,)),
        ],
        compiler_params=pltpu.CompilerParams(
            collective_id=0, has_side_effects=True, vmem_limit_bytes=56 * 2**20
        ),
    )(x, u, wf, wb, channel_bias.reshape(out_chan, 1))
    output = out.transpose(0, 2, 1, 3)
    grad_input = gi.transpose(0, 2, 1, 3)
    weight_grad = wg[: 27 * half].astype(jnp.float32).reshape(27, in_chan * out_chan)
    bias_grad = wg[27 * half, :out_chan].astype(jnp.float32)
    return (output, grad_input, weight_grad, bias_grad)


def solution(mesh):
    n_dp, n_gz = mesh.shape["dp"], mesh.shape["gz"]
    inner_dp = max(d for d in range(1, n_dp + 1) if n_dp % d == 0 and d * d <= n_dp)
    sizes = (inner_dp, n_gz, inner_dp * n_gz, n_dp // inner_dp)
    in_specs = (P("dp", None, "gz", None), P(), P(), P("dp", None, "gz", None))
    out_specs = (P("dp", None, "gz", None), P("dp", None, "gz", None), P(), P())
    return jax.shard_map(
        functools.partial(on_device, sizes),
        mesh=mesh,
        in_specs=in_specs,
        out_specs=out_specs,
        check_vma=False,
    )
```

```python
import functools
import math

import jax
import jax.numpy as jnp
from jax import lax
from jax.experimental import pallas as pl
from jax.experimental.pallas import tpu as pltpu
from jax.sharding import PartitionSpec as P

NX = 64
NY = 8
MESH = pl.DeviceIdType.MESH
LANES = 128
ROWS = 16


def shifted(field):
    cells = field.shape[1]
    at = lax.broadcasted_iota(jnp.int32, field.shape, 1)
    col = at % NX
    zero = jnp.zeros_like(field)
    sides = (
        jnp.where(col == 0, zero, pltpu.roll(field, 1, 1)),
        field,
        jnp.where(col == NX - 1, zero, pltpu.roll(field, cells - 1, 1)),
    )
    found = [jnp.where(at < NX, zero, pltpu.roll(side, NX, 1)) for side in sides]
    found += list(sides)
    found += [jnp.where(at >= cells - NX, zero, pltpu.roll(side, cells - NX, 1)) for side in sides]
    return [each.astype(jnp.bfloat16) for each in found]


def fill(buf, vol, slot, chan, piece, field):
    for tap, value in enumerate(shifted(field)):
        buf[vol, pl.ds((slot * 9 + tap) * chan + piece * ROWS, ROWS), :] = value


def kernel(
    sizes, factor, x_ref, u_ref, taps_ref, bias_ref, out_ref, gi_ref, wg_ref, bg_ref,
    rows_x, rows_u, edge_x, edge_u, taps_rows, wf, wb,
    halo_x, halo_u, near_x, near_u, part, recv_in, acc, recv_out, gath, sums,
    halo_send, halo_recv, in_send, in_recv, out_send, out_recv,
    gout_send, gout_recv, gin_send, gin_recv,
):
    inner_dp, n_gz, n_in, n_out = sizes
    vols, in_chan, planes, cells = x_ref.shape
    out_chan = u_ref.shape[1]
    half = in_chan // 2
    dp, gz = lax.axis_index("dp"), lax.axis_index("gz")
    me_in = lax.rem(dp, inner_dp) * n_gz + gz
    me_out = lax.div(dp, inner_dp)

    def inner_peer(step):
        peer = lax.rem(me_in + step, n_in)
        return peer, {"dp": me_out * inner_dp + lax.div(peer, n_gz), "gz": lax.rem(peer, n_gz)}

    def outer_peer(step):
        peer = lax.rem(me_out + step, n_out)
        return peer, {"dp": peer * inner_dp + lax.rem(dp, inner_dp), "gz": gz}

    tiles = cells // LANES

    def piece_x(vol, z, piece):
        at = pl.ds(piece * planes + z, half, stride=2 * planes)
        return jnp.concatenate([rows_x[vol, tile, at, :] for tile in range(tiles)], axis=1)

    def piece_u(vol, z, piece):
        at = pl.ds(piece * ROWS * planes + z, ROWS, stride=planes)
        return jnp.concatenate([rows_u[vol, tile, at, :] for tile in range(tiles)], axis=1)

    def spread(rows, vol, ref, chan):
        for i in range(chan):
            value = ref[vol, i].astype(jnp.float32)
            for tile in range(tiles):
                at = slice(tile * LANES, (tile + 1) * LANES)
                rows[vol, tile, pl.ds(i * planes, planes), :] = value[:, at]

    def put(rows, vol, at, value):
        for tile in range(tiles):
            rows[vol, tile, at, :] = value[:, tile * LANES : (tile + 1) * LANES]

    def unite(rows, vol, ref, chan):
        for i in range(chan):
            at = pl.ds(i * planes, planes)
            value = jnp.concatenate([rows[vol, tile, at, :] for tile in range(tiles)], axis=1)
            ref[vol, i] = value.astype(jnp.bfloat16)

    barrier = pltpu.get_barrier_semaphore()
    for step in range(1, n_in):
        pl.semaphore_signal(barrier, inc=1, device_id=inner_peer(step)[1], device_id_type=MESH)
    for step in range(1, n_out):
        pl.semaphore_signal(barrier, inc=1, device_id=outer_peer(step)[1], device_id_type=MESH)

    for vol in range(vols):
        spread(rows_x, vol, x_ref, in_chan)
        spread(rows_u, vol, u_ref, out_chan)
        for side, z in ((0, planes - 1), (1, 0)):
            for piece in range(2):
                at = pl.ds(piece * half, half)
                edge_x[side, vol, at, :] = piece_x(vol, z, piece).astype(jnp.bfloat16)
            for piece in range(out_chan // ROWS):
                at = pl.ds(piece * ROWS, ROWS)
                edge_u[side, vol, at, :] = piece_u(vol, z, piece).astype(jnp.bfloat16)

    pl.semaphore_wait(barrier, n_in + n_out - 2)

    def halo_copies(side, which=(0, 1)):
        target = gz + 1 if side == 0 else gz - 1
        return [
            pltpu.make_async_remote_copy(
                src_ref=ref.at[side],
                dst_ref=halo.at[side],
                send_sem=halo_send.at[side, at],
                recv_sem=halo_recv.at[side, at],
                device_id={"gz": target},
                device_id_type=MESH,
            )
            for at, (ref, halo) in enumerate(((edge_x, halo_x), (edge_u, halo_u)))
            if at in which
        ]

    sends = (gz < n_gz - 1, gz > 0)
    gets = (gz > 0, gz < n_gz - 1)
    for side in range(2):

        @pl.when(sends[side])
        def _(side=side):
            for copy in halo_copies(side):
                copy.start()

    deep_x, deep_u = 9 * in_chan, 9 * out_chan
    lanes = (((1,), (1,)), ((), ()))
    for vol in range(vols):
        for z in range(planes):
            for piece in range(2):
                fill(near_x, vol, z + 1, in_chan, piece, piece_x(vol, z, piece))
            for piece in range(out_chan // ROWS):
                fill(near_u, vol, z + 1, out_chan, piece, piece_u(vol, z, piece))

    ones = jnp.ones((8, cells), jnp.bfloat16)
    bias_term = jnp.zeros((8, out_chan), jnp.float32)
    terms = [jnp.zeros((deep_x, out_chan), jnp.float32) for _ in range(3)]

    def grad(vol, z):
        return near_u[vol, pl.ds(((z + 1) * 9 + 4) * out_chan, out_chan), :]

    def pair(vol, z, tap):
        window = near_x[vol, pl.ds((z + tap) * deep_x, deep_x), :]
        return lax.dot_general(window, grad(vol, z), lanes, preferred_element_type=jnp.float32)

    for vol in range(vols):
        for z in range(planes):
            bias_term += lax.dot_general(
                ones, grad(vol, z), lanes, preferred_element_type=jnp.float32
            )
            for tap in range(3):
                if 1 <= z + tap <= planes:
                    terms[tap] += pair(vol, z, tap)

    for side in range(2):

        @pl.when(gets[side])
        def _(side=side):
            halo_copies(side, (0,))[0].wait_recv()

        @pl.when(jnp.logical_not(gets[side]))
        def _(side=side):
            halo_x[side] = jnp.zeros(halo_x.shape[1:], halo_x.dtype)
            halo_u[side] = jnp.zeros(halo_u.shape[1:], halo_u.dtype)

    for vol in range(vols):
        for side, slot in ((0, 0), (1, planes + 1)):
            for piece in range(2):
                field = halo_x[side, vol, pl.ds(piece * half, half), :].astype(jnp.float32)
                fill(near_x, vol, slot, in_chan, piece, field)
        terms[0] += pair(vol, 0, 0)
        terms[2] += pair(vol, planes - 1, 2)
    term = jnp.concatenate(terms, axis=0)
    term = term.reshape(27, 2, half, out_chan)
    term = jnp.concatenate([term[:, 0], term[:, 1]], axis=-1).reshape(27 * half, 2 * out_chan)
    bias_term = jnp.concatenate([bias_term, jnp.zeros_like(bias_term)], axis=-1)
    chunk = part.shape[1]
    filled = 27 * half + 8
    whole = jnp.concatenate(
        [term, bias_term, jnp.zeros((n_in * chunk - filled, LANES), jnp.float32)], axis=0
    )
    part[...] = whole.reshape(part.shape)

    def in_copy(step):
        peer, device = inner_peer(step)
        return pltpu.make_async_remote_copy(
            src_ref=part.at[peer],
            dst_ref=recv_in.at[step - 1],
            send_sem=in_send.at[step - 1],
            recv_sem=in_recv.at[step - 1],
            device_id=device,
            device_id_type=MESH,
        )

    def out_copy(step):
        peer, device = outer_peer(step)
        return pltpu.make_async_remote_copy(
            src_ref=acc.at[peer],
            dst_ref=recv_out.at[step - 1],
            send_sem=out_send.at[step - 1],
            recv_sem=out_recv.at[step - 1],
            device_id=device,
            device_id_type=MESH,
        )

    def gather_out_copy(step):
        return pltpu.make_async_remote_copy(
            src_ref=gath.at[me_in, me_out],
            dst_ref=gath.at[me_in, me_out],
            send_sem=gout_send.at[step - 1],
            recv_sem=gout_recv.at[step - 1],
            device_id=outer_peer(step)[1],
            device_id_type=MESH,
        )

    def gather_in_copy(step):
        return pltpu.make_async_remote_copy(
            src_ref=gath.at[me_in],
            dst_ref=gath.at[me_in],
            send_sem=gin_send.at[step - 1],
            recv_sem=gin_recv.at[step - 1],
            device_id=inner_peer(step)[1],
            device_id_type=MESH,
        )

    for step in range(1, n_in):
        in_copy(step).start()

    stride = taps_rows.shape[0] // half
    for j in range(half):
        taps_rows[pl.ds(j * stride, 27), :] = taps_ref[:, pl.ds(j * LANES, LANES)].astype(jnp.float32)

    def tap_kernel(t):
        both = taps_rows[pl.ds(t, half, stride=stride), :]
        return jnp.concatenate([both[:, :out_chan], both[:, out_chan:]], axis=0)

    group = LANES // in_chan
    for t in range(0, 27, group):
        some = jnp.concatenate([tap_kernel(t + k) for k in range(min(group, 27 - t))], axis=0)
        wf[:, pl.ds(t * in_chan, some.shape[0])] = some.T.astype(jnp.bfloat16)
    for t in range(0, 27, 2):
        some = [tap_kernel(26 - t - k) for k in range(min(2, 27 - t))]
        some = jnp.concatenate(some, axis=1)
        wb[:, pl.ds(t * out_chan, some.shape[1])] = some.astype(jnp.bfloat16)

    rows = (((1,), (0,)), ((), ()))
    bias = jnp.broadcast_to(bias_ref[...], (LANES, out_chan)).T
    bias = jnp.concatenate([bias] * (cells // LANES), axis=1)
    for vol in range(vols):
        for z in range(planes):
            window = near_x[vol, pl.ds(z * deep_x, 3 * deep_x), :]
            value = lax.dot_general(wf[...], window, rows, preferred_element_type=jnp.float32)
            put(rows_u, vol, pl.ds(z, out_chan, stride=planes), value + bias)
        unite(rows_u, vol, out_ref, out_chan)

    for step in range(1, n_in):
        in_copy(step).wait_recv()
    total = part[me_in]
    for step in range(1, n_in):
        total += recv_in[step - 1]
    acc[...] = total.reshape(acc.shape)
    for step in range(1, n_out):
        out_copy(step).start()

    for side in range(2):

        @pl.when(gets[side])
        def _(side=side):
            halo_copies(side, (1,))[0].wait_recv()

    for vol in range(vols):
        for side, slot in ((0, 0), (1, planes + 1)):
            for piece in range(out_chan // ROWS):
                field = halo_u[side, vol, pl.ds(piece * ROWS, ROWS), :].astype(jnp.float32)
                fill(near_u, vol, slot, out_chan, piece, field)
    for vol in range(vols):
        for z in range(planes):
            window = near_u[vol, pl.ds(z * deep_u, 3 * deep_u), :]
            value = lax.dot_general(wb[...], window, rows, preferred_element_type=jnp.float32)
            for piece in range(2):
                at = pl.ds(piece * planes + z, half, stride=2 * planes)
                put(rows_x, vol, at, value[piece * half : (piece + 1) * half])
        unite(rows_x, vol, gi_ref, in_chan)

    for step in range(1, n_out):
        out_copy(step).wait_recv()
    total = acc[me_out]
    for step in range(1, n_out):
        total += recv_out[step - 1]
    gath[me_in, me_out] = (total * factor).astype(jnp.bfloat16)
    for step in range(1, n_out):
        gather_out_copy(step).start()
    for step in range(1, n_out):
        gather_out_copy(step).wait_recv()
    for step in range(1, n_in):
        gather_in_copy(step).start()
    for step in range(1, n_in):
        gather_in_copy(step).wait_recv()
    sums[...] = gath[...].astype(jnp.float32).reshape(sums.shape)
    for j in range(half):
        wg_ref[:, pl.ds(j * LANES, LANES)] = sums[pl.ds(j, 27, stride=half), :]
    bg_ref[...] = sums[pl.ds(27 * half, 1), :out_chan]

    for side in range(2):

        @pl.when(sends[side])
        def _(side=side):
            for copy in halo_copies(side):
                copy.wait_send()

    for step in range(1, n_in):
        in_copy(step).wait_send()
        gather_in_copy(step).wait_send()
    for step in range(1, n_out):
        out_copy(step).wait_send()
        gather_out_copy(step).wait_send()


def on_device(sizes, features_in, kernel_taps, channel_bias, upstream):
    inner_dp, n_gz, n_in, n_out = sizes
    vols, in_chan, planes, cells = features_in.shape
    out_chan = upstream.shape[1]
    half = in_chan // 2
    cells_all = vols * inner_dp * n_out * planes * n_gz * cells
    factor = 1.0 / math.sqrt(cells_all)
    filled = 27 * half + 8
    per = ROWS * -(-filled // (ROWS * n_in * n_out))
    vmem = pl.BlockSpec(memory_space=pltpu.VMEM)
    dma = pltpu.SemaphoreType.DMA
    steps_in, steps_out = max(n_in - 1, 1), max(n_out - 1, 1)
    output, grad_input, weight_grad, bias_grad = pl.pallas_call(
        functools.partial(kernel, sizes, factor),
        out_shape=(
            jax.ShapeDtypeStruct(upstream.shape, jnp.bfloat16),
            jax.ShapeDtypeStruct(features_in.shape, jnp.bfloat16),
            jax.ShapeDtypeStruct(kernel_taps.shape, jnp.float32),
            jax.ShapeDtypeStruct((1, out_chan), jnp.float32),
        ),
        in_specs=[vmem] * 4,
        out_specs=(vmem,) * 4,
        scratch_shapes=[
            pltpu.VMEM((vols, cells // LANES, in_chan * planes, LANES), jnp.float32),
            pltpu.VMEM((vols, cells // LANES, out_chan * planes, LANES), jnp.float32),
            pltpu.VMEM((2, vols, in_chan, cells), jnp.bfloat16),
            pltpu.VMEM((2, vols, out_chan, cells), jnp.bfloat16),
            pltpu.VMEM((32 * half, LANES), jnp.float32),
            pltpu.VMEM((out_chan, 27 * in_chan), jnp.bfloat16),
            pltpu.VMEM((in_chan, 27 * out_chan), jnp.bfloat16),
            pltpu.VMEM((2, vols, in_chan, cells), jnp.bfloat16),
            pltpu.VMEM((2, vols, out_chan, cells), jnp.bfloat16),
            pltpu.VMEM((vols, (planes + 2) * 9 * in_chan, cells), jnp.bfloat16),
            pltpu.VMEM((vols, (planes + 2) * 9 * out_chan, cells), jnp.bfloat16),
            pltpu.VMEM((n_in, n_out * per, LANES), jnp.float32),
            pltpu.VMEM((steps_in, n_out * per, LANES), jnp.float32),
            pltpu.VMEM((n_out, per, LANES), jnp.float32),
            pltpu.VMEM((steps_out, per, LANES), jnp.float32),
            pltpu.VMEM((n_in, n_out, per, LANES), jnp.bfloat16),
            pltpu.VMEM((n_in * n_out * per, LANES), jnp.float32),
            dma((2, 2)),
            dma((2, 2)),
            dma((steps_in,)),
            dma((steps_in,)),
            dma((steps_out,)),
            dma((steps_out,)),
            dma((steps_out,)),
            dma((steps_out,)),
            dma((steps_in,)),
            dma((steps_in,)),
        ],
        compiler_params=pltpu.CompilerParams(
            collective_id=0, has_side_effects=True, vmem_limit_bytes=56 * 2**20
        ),
    )(features_in, upstream, kernel_taps, channel_bias.reshape(1, out_chan))
    return (output, grad_input, weight_grad, bias_grad.reshape(out_chan))


def solution(mesh):
    n_dp, n_gz = mesh.shape["dp"], mesh.shape["gz"]
    inner_dp = max(d for d in range(1, n_dp + 1) if n_dp % d == 0 and d * d <= n_dp)
    sizes = (inner_dp, n_gz, inner_dp * n_gz, n_dp // inner_dp)
    in_specs = (P("dp", None, "gz", None), P(), P(), P("dp", None, "gz", None))
    out_specs = (P("dp", None, "gz", None), P("dp", None, "gz", None), P(), P())
    return jax.shard_map(
        functools.partial(on_device, sizes),
        mesh=mesh,
        in_specs=in_specs,
        out_specs=out_specs,
        check_vma=False,
    )
```

```python
import functools
import math

import jax
import jax.numpy as jnp
from jax import lax
from jax.experimental import pallas as pl
from jax.experimental.pallas import tpu as pltpu
from jax.sharding import PartitionSpec as P

NX = 64
NY = 8
MESH = pl.DeviceIdType.MESH
LANES = 128
ROWS = 16


def shifted(field):
    cells = field.shape[1]
    at = lax.broadcasted_iota(jnp.int32, field.shape, 1)
    col = at % NX
    zero = jnp.zeros_like(field)
    sides = (
        jnp.where(col == 0, zero, pltpu.roll(field, 1, 1)),
        field,
        jnp.where(col == NX - 1, zero, pltpu.roll(field, cells - 1, 1)),
    )
    found = [jnp.where(at < NX, zero, pltpu.roll(side, NX, 1)) for side in sides]
    found += list(sides)
    found += [jnp.where(at >= cells - NX, zero, pltpu.roll(side, cells - NX, 1)) for side in sides]
    return [each.astype(jnp.bfloat16) for each in found]


def fill(buf, vol, start, chan, piece, field):
    for tap, value in enumerate(shifted(field)):
        buf[vol, pl.ds(start + tap * chan + piece * ROWS, ROWS), :] = value


def depth(chan):
    return LANES * -(-9 * chan // LANES)


def kernel(
    sizes, factor, x_hbm, u_hbm, taps_hbm, bias_ref, out_ref, gi_ref, wg_ref, bg_ref,
    x_ref, u_ref, taps_ref, load, rows_x, rows_u, edge_x, edge_u, taps_rows, wf, wb,
    halo_x, halo_u, near_x, near_u, part, recv_in, acc, recv_out, gath, sums,
    halo_send, halo_recv, in_send, in_recv, out_send, out_recv,
    gout_send, gout_recv, gin_send, gin_recv,
):
    inner_dp, n_gz, n_in, n_out = sizes
    vols, in_chan, planes, cells = x_ref.shape
    out_chan = u_ref.shape[1]
    half = in_chan // 2
    dp, gz = lax.axis_index("dp"), lax.axis_index("gz")
    me_in = lax.rem(dp, inner_dp) * n_gz + gz
    me_out = lax.div(dp, inner_dp)

    def inner_peer(step):
        peer = lax.rem(me_in + step, n_in)
        return peer, {"dp": me_out * inner_dp + lax.div(peer, n_gz), "gz": lax.rem(peer, n_gz)}

    def outer_peer(step):
        peer = lax.rem(me_out + step, n_out)
        return peer, {"dp": peer * inner_dp + lax.rem(dp, inner_dp), "gz": gz}

    tiles = cells // LANES

    def piece_x(vol, z, piece):
        at = pl.ds(piece * planes + z, half, stride=2 * planes)
        return jnp.concatenate([rows_x[vol, tile, at, :] for tile in range(tiles)], axis=1)

    def piece_u(vol, z, piece):
        at = pl.ds(piece * ROWS * planes + z, ROWS, stride=planes)
        return jnp.concatenate([rows_u[vol, tile, at, :] for tile in range(tiles)], axis=1)

    def spread(rows, vol, ref, chan):
        for i in range(chan):
            value = ref[vol, i].astype(jnp.float32)
            for tile in range(tiles):
                at = slice(tile * LANES, (tile + 1) * LANES)
                rows[vol, tile, pl.ds(i * planes, planes), :] = value[:, at]

    def put(rows, vol, at, value):
        for tile in range(tiles):
            rows[vol, tile, at, :] = value[:, tile * LANES : (tile + 1) * LANES]

    def unite(rows, vol, ref, chan):
        for i in range(chan):
            at = pl.ds(i * planes, planes)
            value = jnp.concatenate([rows[vol, tile, at, :] for tile in range(tiles)], axis=1)
            ref[vol, i] = value.astype(jnp.bfloat16)

    loads = [
        pltpu.make_async_copy(source, target, load.at[at])
        for at, (source, target) in enumerate(((x_hbm, x_ref), (u_hbm, u_ref), (taps_hbm, taps_ref)))
    ]
    for copy in loads:
        copy.start()
    barrier = pltpu.get_barrier_semaphore()
    for step in range(1, n_in):
        pl.semaphore_signal(barrier, inc=1, device_id=inner_peer(step)[1], device_id_type=MESH)
    for step in range(1, n_out):
        pl.semaphore_signal(barrier, inc=1, device_id=outer_peer(step)[1], device_id_type=MESH)

    deep_x, deep_u = 9 * in_chan, depth(out_chan)
    loads[0].wait()
    for vol in range(vols):
        spread(rows_x, vol, x_ref, in_chan)
        for side, z in ((0, planes - 1), (1, 0)):
            for piece in range(2):
                at = pl.ds(piece * half, half)
                edge_x[side, vol, at, :] = piece_x(vol, z, piece).astype(jnp.bfloat16)

    pl.semaphore_wait(barrier, n_in + n_out - 2)

    def halo_copies(side, which=(0, 1)):
        target = gz + 1 if side == 0 else gz - 1
        return [
            pltpu.make_async_remote_copy(
                src_ref=ref.at[side],
                dst_ref=halo.at[side],
                send_sem=halo_send.at[side, at],
                recv_sem=halo_recv.at[side, at],
                device_id={"gz": target},
                device_id_type=MESH,
            )
            for at, (ref, halo) in enumerate(((edge_x, halo_x), (edge_u, halo_u)))
            if at in which
        ]

    sends = (gz < n_gz - 1, gz > 0)
    gets = (gz > 0, gz < n_gz - 1)
    def send_halos(which):
        for side in range(2):

            @pl.when(sends[side])
            def _(side=side):
                halo_copies(side, (which,))[0].start()

    def center(slot):
        return slot * deep_u + 4 * out_chan

    send_halos(0)
    loads[1].wait()
    for vol in range(vols):
        spread(rows_u, vol, u_ref, out_chan)
        for z in range(planes):
            for piece in range(out_chan // ROWS):
                value = piece_u(vol, z, piece).astype(jnp.bfloat16)
                near_u[vol, pl.ds(center(z + 1) + piece * ROWS, ROWS), :] = value
        for side, z in ((0, planes - 1), (1, 0)):
            edge_u[side, vol] = near_u[vol, pl.ds(center(z + 1), out_chan), :]
    send_halos(1)
    lanes = (((1,), (1,)), ((), ()))
    for vol in range(vols):
        for z in range(planes):
            for piece in range(2):
                fill(near_x, vol, (z + 1) * deep_x, in_chan, piece, piece_x(vol, z, piece))

    ones = jnp.ones((8, cells), jnp.bfloat16)
    bias_term = jnp.zeros((8, out_chan), jnp.float32)
    terms = [jnp.zeros((deep_x, out_chan), jnp.float32) for _ in range(3)]

    def grad(vol, z):
        return near_u[vol, pl.ds(center(z + 1), out_chan), :]

    def pair(vol, z, tap):
        window = near_x[vol, pl.ds((z + tap) * deep_x, deep_x), :]
        return lax.dot_general(window, grad(vol, z), lanes, preferred_element_type=jnp.float32)

    for vol in range(vols):
        for z in range(planes):
            bias_term += lax.dot_general(
                ones, grad(vol, z), lanes, preferred_element_type=jnp.float32
            )
            for tap in range(3):
                if 1 <= z + tap <= planes:
                    terms[tap] += pair(vol, z, tap)

    for side in range(2):

        @pl.when(gets[side])
        def _(side=side):
            halo_copies(side, (0,))[0].wait_recv()

        @pl.when(jnp.logical_not(gets[side]))
        def _(side=side):
            halo_x[side] = jnp.zeros(halo_x.shape[1:], halo_x.dtype)
            halo_u[side] = jnp.zeros(halo_u.shape[1:], halo_u.dtype)

    for vol in range(vols):
        for side, slot in ((0, 0), (1, planes + 1)):
            for piece in range(2):
                field = halo_x[side, vol, pl.ds(piece * half, half), :].astype(jnp.float32)
                fill(near_x, vol, slot * deep_x, in_chan, piece, field)
        terms[0] += pair(vol, 0, 0)
        terms[2] += pair(vol, planes - 1, 2)
    term = jnp.concatenate(terms, axis=0)
    term = term.reshape(27, 2, half, out_chan)
    term = jnp.concatenate([term[:, 0], term[:, 1]], axis=-1).reshape(27 * half, 2 * out_chan)
    bias_term = jnp.concatenate([bias_term, jnp.zeros_like(bias_term)], axis=-1)
    chunk = part.shape[1]
    filled = 27 * half + 8
    whole = jnp.concatenate(
        [term, bias_term, jnp.zeros((n_in * chunk - filled, LANES), jnp.float32)], axis=0
    )
    part[...] = whole.reshape(part.shape)

    def in_copy(step):
        peer, device = inner_peer(step)
        return pltpu.make_async_remote_copy(
            src_ref=part.at[peer],
            dst_ref=recv_in.at[step - 1],
            send_sem=in_send.at[step - 1],
            recv_sem=in_recv.at[step - 1],
            device_id=device,
            device_id_type=MESH,
        )

    def out_copy(step):
        peer, device = outer_peer(step)
        return pltpu.make_async_remote_copy(
            src_ref=acc.at[peer],
            dst_ref=recv_out.at[step - 1],
            send_sem=out_send.at[step - 1],
            recv_sem=out_recv.at[step - 1],
            device_id=device,
            device_id_type=MESH,
        )

    def gather_out_copy(step):
        return pltpu.make_async_remote_copy(
            src_ref=gath.at[me_in, me_out],
            dst_ref=gath.at[me_in, me_out],
            send_sem=gout_send.at[step - 1],
            recv_sem=gout_recv.at[step - 1],
            device_id=outer_peer(step)[1],
            device_id_type=MESH,
        )

    def gather_in_copy(step):
        return pltpu.make_async_remote_copy(
            src_ref=gath.at[me_in],
            dst_ref=gath.at[me_in],
            send_sem=gin_send.at[step - 1],
            recv_sem=gin_recv.at[step - 1],
            device_id=inner_peer(step)[1],
            device_id_type=MESH,
        )

    for step in range(1, n_in):
        in_copy(step).start()

    loads[2].wait()
    stride = taps_rows.shape[0] // half
    for j in range(half):
        taps_rows[pl.ds(j * stride, 27), :] = taps_ref[:, pl.ds(j * LANES, LANES)].astype(jnp.float32)

    def tap_kernel(t):
        both = taps_rows[pl.ds(t, half, stride=stride), :]
        return jnp.concatenate([both[:, :out_chan], both[:, out_chan:]], axis=0)

    group = LANES // in_chan
    for t in range(0, 27, group):
        some = jnp.concatenate([tap_kernel(t + k) for k in range(min(group, 27 - t))], axis=0)
        wf[:, pl.ds(t * in_chan, some.shape[0])] = some.T.astype(jnp.bfloat16)
    wb[...] = jnp.zeros_like(wb)
    for a in range(3):
        for t in range(0, 9, 2):
            some = [tap_kernel(26 - 9 * a - t - k) for k in range(min(2, 9 - t))]
            some = jnp.concatenate(some, axis=1).astype(jnp.bfloat16)
            for z in range(planes):
                at = pl.ds((z + a) * deep_u + t * out_chan, some.shape[1])
                wb[pl.ds(z * in_chan, in_chan), at] = some

    pad = deep_u - 9 * out_chan
    for vol in range(vols):
        if pad:
            for slot in range(planes + 2):
                at = pl.ds(slot * deep_u + 9 * out_chan, pad)
                near_u[vol, at, :] = jnp.zeros((pad, cells), jnp.bfloat16)
        for z in range(planes):
            for piece in range(out_chan // ROWS):
                fill(near_u, vol, (z + 1) * deep_u, out_chan, piece, piece_u(vol, z, piece))

    rows = (((1,), (0,)), ((), ()))
    bias = jnp.broadcast_to(bias_ref[...], (LANES, out_chan)).T
    bias = jnp.concatenate([bias] * (cells // LANES), axis=1)
    for vol in range(vols):
        for z in range(planes):
            window = near_x[vol, pl.ds(z * deep_x, 3 * deep_x), :]
            value = lax.dot_general(wf[...], window, rows, preferred_element_type=jnp.float32)
            put(rows_u, vol, pl.ds(z, out_chan, stride=planes), value + bias)
    for step in range(1, n_in):
        in_copy(step).wait_recv()
    total = part[me_in]
    for step in range(1, n_in):
        total += recv_in[step - 1]
    acc[...] = total.reshape(acc.shape)
    for step in range(1, n_out):
        out_copy(step).start()

    for side in range(2):

        @pl.when(gets[side])
        def _(side=side):
            halo_copies(side, (1,))[0].wait_recv()

    for vol in range(vols):
        for side, slot in ((0, 0), (1, planes + 1)):
            for piece in range(out_chan // ROWS):
                field = halo_u[side, vol, pl.ds(piece * ROWS, ROWS), :].astype(jnp.float32)
                fill(near_u, vol, slot * deep_u, out_chan, piece, field)
    for vol in range(vols):
        unite(rows_u, vol, out_ref, out_chan)

    def backward(first):
        tile = min(2 * LANES, cells)
        for vol in range(vols):
            for at in range(0 if first else tile, tile if first else cells, tile):
                field = near_u[vol, :, pl.ds(at, tile)]
                value = lax.dot_general(wb[...], field, rows, preferred_element_type=jnp.float32)
                for z in range(planes):
                    for piece in range(2):
                        low = z * in_chan + piece * half
                        out = pl.ds(piece * planes + z, half, stride=2 * planes)
                        for k in range(tile // LANES):
                            part_k = value[low : low + half, k * LANES : (k + 1) * LANES]
                            rows_x[vol, at // LANES + k, out, :] = part_k

    for step in range(1, n_out):
        out_copy(step).wait_recv()
    total = acc[me_out]
    for step in range(1, n_out):
        total += recv_out[step - 1]
    gath[me_in, me_out] = (total * factor).astype(jnp.bfloat16)
    for step in range(1, n_out):
        gather_out_copy(step).start()
    backward(True)
    for step in range(1, n_out):
        gather_out_copy(step).wait_recv()
    for step in range(1, n_in):
        gather_in_copy(step).start()
    backward(False)
    for vol in range(vols):
        unite(rows_x, vol, gi_ref, in_chan)
    for step in range(1, n_in):
        gather_in_copy(step).wait_recv()
    sums[...] = gath[...].astype(jnp.float32).reshape(sums.shape)
    for j in range(half):
        wg_ref[:, pl.ds(j * LANES, LANES)] = sums[pl.ds(j, 27, stride=half), :]
    bg_ref[...] = sums[pl.ds(27 * half, 1), :out_chan]

    for side in range(2):

        @pl.when(sends[side])
        def _(side=side):
            for copy in halo_copies(side):
                copy.wait_send()

    for step in range(1, n_in):
        in_copy(step).wait_send()
        gather_in_copy(step).wait_send()
    for step in range(1, n_out):
        out_copy(step).wait_send()
        gather_out_copy(step).wait_send()


def finish(*refs):
    sem = refs[8]
    copies = [pltpu.make_async_copy(refs[k], refs[4 + k], sem.at[k]) for k in range(4)]
    for copy in copies:
        copy.start()
    for copy in copies:
        copy.wait()


def on_device(sizes, features_in, kernel_taps, channel_bias, upstream):
    inner_dp, n_gz, n_in, n_out = sizes
    vols, in_chan, planes, cells = features_in.shape
    out_chan = upstream.shape[1]
    half = in_chan // 2
    cells_all = vols * inner_dp * n_out * planes * n_gz * cells
    factor = 1.0 / math.sqrt(cells_all)
    filled = 27 * half + 8
    per = ROWS * -(-filled // (ROWS * n_in * n_out))
    vmem = pl.BlockSpec(memory_space=pltpu.VMEM)
    hbm = pl.BlockSpec(memory_space=pltpu.HBM)
    dma = pltpu.SemaphoreType.DMA
    steps_in, steps_out = max(n_in - 1, 1), max(n_out - 1, 1)
    scratch = [
        pltpu.VMEM(features_in.shape, jnp.bfloat16),
        pltpu.VMEM(upstream.shape, jnp.bfloat16),
        pltpu.VMEM(kernel_taps.shape, jnp.bfloat16),
        dma((3,)),
        pltpu.VMEM((vols, cells // LANES, in_chan * planes, LANES), jnp.float32),
        pltpu.VMEM((vols, cells // LANES, out_chan * planes, LANES), jnp.float32),
        pltpu.VMEM((2, vols, in_chan, cells), jnp.bfloat16),
        pltpu.VMEM((2, vols, out_chan, cells), jnp.bfloat16),
        pltpu.VMEM((32 * half, LANES), jnp.float32),
        pltpu.VMEM((out_chan, 27 * in_chan), jnp.bfloat16),
        pltpu.VMEM((planes * in_chan, (planes + 2) * depth(out_chan)), jnp.bfloat16),
        pltpu.VMEM((2, vols, in_chan, cells), jnp.bfloat16),
        pltpu.VMEM((2, vols, out_chan, cells), jnp.bfloat16),
        pltpu.VMEM((vols, (planes + 2) * 9 * in_chan, cells), jnp.bfloat16),
        pltpu.VMEM((vols, (planes + 2) * depth(out_chan), cells), jnp.bfloat16),
        pltpu.VMEM((n_in, n_out * per, LANES), jnp.float32),
        pltpu.VMEM((steps_in, n_out * per, LANES), jnp.float32),
        pltpu.VMEM((n_out, per, LANES), jnp.float32),
        pltpu.VMEM((steps_out, per, LANES), jnp.float32),
        pltpu.VMEM((n_in, n_out, per, LANES), jnp.bfloat16),
        pltpu.VMEM((n_in * n_out * per, LANES), jnp.float32),
        dma((2, 2)),
        dma((2, 2)),
        dma((steps_in,)),
        dma((steps_in,)),
        dma((steps_out,)),
        dma((steps_out,)),
        dma((steps_out,)),
        dma((steps_out,)),
        dma((steps_in,)),
        dma((steps_in,)),
    ]
    held = [each for each in scratch if each.memory_space == pltpu.VMEM]
    grant = sum(math.prod(each.shape) * jnp.dtype(each.dtype).itemsize for each in held)
    results = pl.pallas_call(
        functools.partial(kernel, sizes, factor),
        out_shape=(
            jax.ShapeDtypeStruct(upstream.shape, jnp.bfloat16),
            jax.ShapeDtypeStruct(features_in.shape, jnp.bfloat16),
            jax.ShapeDtypeStruct(kernel_taps.shape, jnp.float32),
            jax.ShapeDtypeStruct((1, out_chan), jnp.float32),
        ),
        in_specs=[hbm, hbm, hbm, vmem],
        out_specs=(vmem,) * 4,
        scratch_shapes=scratch,
        compiler_params=pltpu.CompilerParams(
            collective_id=0, has_side_effects=True, vmem_limit_bytes=grant + 6 * 2**20
        ),
    )(features_in, upstream, kernel_taps, channel_bias.reshape(1, out_chan))
    output, grad_input, weight_grad, bias_grad = pl.pallas_call(
        finish,
        out_shape=tuple(jax.ShapeDtypeStruct(each.shape, each.dtype) for each in results),
        in_specs=[vmem] * 4,
        out_specs=(hbm,) * 4,
        scratch_shapes=[dma((4,))],
        compiler_params=pltpu.CompilerParams(vmem_limit_bytes=4 * 2**20),
    )(*results)
    return (output, grad_input, weight_grad, bias_grad.reshape(out_chan))


def solution(mesh):
    n_dp, n_gz = mesh.shape["dp"], mesh.shape["gz"]
    inner_dp = max(d for d in range(1, n_dp + 1) if n_dp % d == 0 and d * d <= n_dp)
    sizes = (inner_dp, n_gz, inner_dp * n_gz, n_dp // inner_dp)
    in_specs = (P("dp", None, "gz", None), P(), P(), P("dp", None, "gz", None))
    out_specs = (P("dp", None, "gz", None), P("dp", None, "gz", None), P(), P())
    return jax.shard_map(
        functools.partial(on_device, sizes),
        mesh=mesh,
        in_specs=in_specs,
        out_specs=out_specs,
        check_vma=False,
    )
```

```python
import functools
import math

import jax
import jax.numpy as jnp
from jax import lax
from jax.experimental import pallas as pl
from jax.experimental.pallas import tpu as pltpu
from jax.sharding import PartitionSpec as P

NX = 64
NY = 8
MESH = pl.DeviceIdType.MESH
LANES = 128
ROWS = 16


def shifted(field):
    cells = field.shape[1]
    at = lax.broadcasted_iota(jnp.int32, field.shape, 1)
    col = at % NX
    zero = jnp.zeros_like(field)
    sides = (
        jnp.where(col == 0, zero, pltpu.roll(field, 1, 1)),
        field,
        jnp.where(col == NX - 1, zero, pltpu.roll(field, cells - 1, 1)),
    )
    found = [jnp.where(at < NX, zero, pltpu.roll(side, NX, 1)) for side in sides]
    found += list(sides)
    found += [jnp.where(at >= cells - NX, zero, pltpu.roll(side, cells - NX, 1)) for side in sides]
    return [each.astype(jnp.bfloat16) for each in found]


def fill(buf, vol, start, chan, piece, field):
    for tap, value in enumerate(shifted(field)):
        buf[vol, pl.ds(start + tap * chan + piece * ROWS, ROWS), :] = value


def depth(chan):
    return LANES * -(-9 * chan // LANES)


def kernel(
    sizes, factor, x_hbm, u_hbm, taps_hbm, bias_hbm, out_ref, gi_ref, wg_ref, bg_ref,
    x_ref, u_ref, taps_ref, bias_ref, load, grads, rows_x, rows_u, edge_x, edge_u, taps_rows, wf, wb,
    halo_x, halo_u, near_x, near_u, part_a, part_b, recv_a, recv_b, acc, recv_out, gath,
    sums_a, sums_b,
    halo_send, halo_recv, in_send, in_recv, out_send, out_recv,
    gout_send, gout_recv, gin_send, gin_recv,
):
    inner_dp, n_gz, n_in, n_out = sizes
    vols, in_chan, planes, cells = x_ref.shape
    out_chan = u_ref.shape[1]
    half = in_chan // 2
    dp, gz = lax.axis_index("dp"), lax.axis_index("gz")
    me_in = lax.rem(dp, inner_dp) * n_gz + gz
    me_out = lax.div(dp, inner_dp)

    def inner_peer(step):
        peer = lax.rem(me_in + step, n_in)
        return peer, {"dp": me_out * inner_dp + lax.div(peer, n_gz), "gz": lax.rem(peer, n_gz)}

    def outer_peer(step):
        peer = lax.rem(me_out + step, n_out)
        return peer, {"dp": peer * inner_dp + lax.rem(dp, inner_dp), "gz": gz}

    tiles = cells // LANES

    def piece_x(vol, z, piece):
        at = pl.ds(piece * planes + z, half, stride=2 * planes)
        return jnp.concatenate([rows_x[vol, tile, at, :] for tile in range(tiles)], axis=1)

    def piece_u(vol, z, piece):
        at = pl.ds(piece * ROWS * planes + z, ROWS, stride=planes)
        return jnp.concatenate([rows_u[vol, tile, at, :] for tile in range(tiles)], axis=1)

    def spread(rows, vol, ref, chan):
        for i in range(chan):
            value = ref[vol, i].astype(jnp.float32)
            for tile in range(tiles):
                at = slice(tile * LANES, (tile + 1) * LANES)
                rows[vol, tile, pl.ds(i * planes, planes), :] = value[:, at]

    def put(rows, vol, at, value):
        for tile in range(tiles):
            rows[vol, tile, at, :] = value[:, tile * LANES : (tile + 1) * LANES]

    def unite(rows, vol, ref, chan):
        for i in range(chan):
            at = pl.ds(i * planes, planes)
            value = jnp.concatenate([rows[vol, tile, at, :] for tile in range(tiles)], axis=1)
            ref[vol, i] = value.astype(jnp.bfloat16)

    moves = ((x_hbm, x_ref), (u_hbm, u_ref), (taps_hbm, taps_ref), (bias_hbm, bias_ref))
    loads = [
        pltpu.make_async_copy(source, target, load.at[at])
        for at, (source, target) in enumerate(moves)
    ]
    for copy in loads:
        copy.start()
    barrier = pltpu.get_barrier_semaphore()
    for step in range(1, n_in):
        pl.semaphore_signal(barrier, inc=1, device_id=inner_peer(step)[1], device_id_type=MESH)
    for step in range(1, n_out):
        pl.semaphore_signal(barrier, inc=1, device_id=outer_peer(step)[1], device_id_type=MESH)

    deep_x, deep_u = 9 * in_chan, depth(out_chan)
    loads[0].wait()
    for vol in range(vols):
        spread(rows_x, vol, x_ref, in_chan)
        for side, z in ((0, planes - 1), (1, 0)):
            for piece in range(2):
                at = pl.ds(piece * half, half)
                edge_x[side, vol, at, :] = piece_x(vol, z, piece).astype(jnp.bfloat16)

    pl.semaphore_wait(barrier, n_in + n_out - 2)

    def halo_copies(side, which=(0, 1)):
        target = gz + 1 if side == 0 else gz - 1
        return [
            pltpu.make_async_remote_copy(
                src_ref=ref.at[side],
                dst_ref=halo.at[side],
                send_sem=halo_send.at[side, at],
                recv_sem=halo_recv.at[side, at],
                device_id={"gz": target},
                device_id_type=MESH,
            )
            for at, (ref, halo) in enumerate(((edge_x, halo_x), (edge_u, halo_u)))
            if at in which
        ]

    sends = (gz < n_gz - 1, gz > 0)
    gets = (gz > 0, gz < n_gz - 1)
    def send_halos(which):
        for side in range(2):

            @pl.when(sends[side])
            def _(side=side):
                halo_copies(side, (which,))[0].start()

    send_halos(0)
    loads[1].wait()
    for vol in range(vols):
        spread(rows_u, vol, u_ref, out_chan)
        for z in range(planes):
            for piece in range(out_chan // ROWS):
                value = piece_u(vol, z, piece).astype(jnp.bfloat16)
                grads[vol, pl.ds(z * out_chan + piece * ROWS, ROWS), :] = value
        for side, z in ((0, planes - 1), (1, 0)):
            edge_u[side, vol] = grads[vol, pl.ds(z * out_chan, out_chan), :]
    send_halos(1)
    lanes = (((1,), (1,)), ((), ()))
    for vol in range(vols):
        for z in range(planes):
            for piece in range(2):
                fill(near_x, vol, (z + 1) * deep_x, in_chan, piece, piece_x(vol, z, piece))

    def product(vol, slot, count, at, wide):
        window = near_x[vol, pl.ds(slot * deep_x, count * deep_x), :]
        grad = grads[vol, pl.ds(at, wide), :]
        return lax.dot_general(window, grad, lanes, preferred_element_type=jnp.float32)

    def lane_tile(value, k):
        return value[:, k * LANES : (k + 1) * LANES]

    last = planes * out_chan - LANES
    even = [jnp.zeros((deep_x, LANES), jnp.float32) for _ in range(3)]
    odd = [jnp.zeros((deep_x, LANES), jnp.float32) for _ in range(3)]
    ones = jnp.ones((8, cells), jnp.bfloat16)
    bias_term = jnp.zeros((8, LANES), jnp.float32)
    for vol in range(vols):
        inside = product(vol, 1, planes, 0, planes * out_chan)
        for tap in range(3):
            for z in range(planes):
                if 1 <= z + tap <= planes:
                    low = (z + tap - 1) * deep_x
                    kept = odd if z % 2 else even
                    kept[tap] += lane_tile(inside[low : low + deep_x], z // 2)
        bias_all = lax.dot_general(
            ones, grads[vol], lanes, preferred_element_type=jnp.float32
        )
        for k in range(planes // 2):
            bias_term += lane_tile(bias_all, k)

    def packed(tap):
        first = even[tap].reshape(9, 2, half, LANES)
        second = odd[tap].reshape(9, 2, half, LANES)
        low = lax.broadcasted_iota(jnp.int32, (9, half, LANES), 2) < out_chan
        stay = jnp.where(low, first[:, 0], second[:, 1]).reshape(9 * half, LANES)
        move = jnp.where(low, first[:, 1], second[:, 0]).reshape(9 * half, LANES)
        return stay + pltpu.roll(move, out_chan, 1)

    def lay(part, pieces):
        rest = math.prod(part.shape[:2]) - sum(each.shape[0] for each in pieces)
        if rest:
            pieces = pieces + [jnp.zeros((rest, LANES), jnp.float32)]
        part[...] = jnp.concatenate(pieces, axis=0).reshape(part.shape)

    def in_copy(step, second):
        peer, device = inner_peer(step)
        return pltpu.make_async_remote_copy(
            src_ref=(part_b if second else part_a).at[peer],
            dst_ref=(recv_b if second else recv_a).at[step - 1],
            send_sem=in_send.at[second, step - 1],
            recv_sem=in_recv.at[second, step - 1],
            device_id=device,
            device_id_type=MESH,
        )

    bias_term += pltpu.roll(bias_term, out_chan, 1)
    lay(part_a, [packed(1), bias_term])
    for step in range(1, n_in):
        in_copy(step, 0).start()

    for side in range(2):

        @pl.when(gets[side])
        def _(side=side):
            halo_copies(side, (0,))[0].wait_recv()

        @pl.when(jnp.logical_not(gets[side]))
        def _(side=side):
            halo_x[side] = jnp.zeros(halo_x.shape[1:], halo_x.dtype)
            halo_u[side] = jnp.zeros(halo_u.shape[1:], halo_u.dtype)

    for vol in range(vols):
        for side, slot in ((0, 0), (1, planes + 1)):
            for piece in range(2):
                field = halo_x[side, vol, pl.ds(piece * half, half), :].astype(jnp.float32)
                fill(near_x, vol, slot * deep_x, in_chan, piece, field)
        even[0] += product(vol, 0, 1, 0, LANES)
        odd[2] += product(vol, planes + 1, 1, last, LANES)
    lay(part_b, [packed(0), packed(2)])
    for step in range(1, n_in):
        in_copy(step, 1).start()

    def out_copy(step):
        peer, device = outer_peer(step)
        return pltpu.make_async_remote_copy(
            src_ref=acc.at[peer],
            dst_ref=recv_out.at[step - 1],
            send_sem=out_send.at[step - 1],
            recv_sem=out_recv.at[step - 1],
            device_id=device,
            device_id_type=MESH,
        )

    def gather_out_copy(step):
        return pltpu.make_async_remote_copy(
            src_ref=gath.at[me_in, me_out],
            dst_ref=gath.at[me_in, me_out],
            send_sem=gout_send.at[step - 1],
            recv_sem=gout_recv.at[step - 1],
            device_id=outer_peer(step)[1],
            device_id_type=MESH,
        )

    def gather_in_copy(step):
        return pltpu.make_async_remote_copy(
            src_ref=gath.at[me_in],
            dst_ref=gath.at[me_in],
            send_sem=gin_send.at[step - 1],
            recv_sem=gin_recv.at[step - 1],
            device_id=inner_peer(step)[1],
            device_id_type=MESH,
        )

    loads[2].wait()
    loads[3].wait()
    stride = taps_rows.shape[0] // half
    for j in range(half):
        taps_rows[pl.ds(j * stride, 27), :] = taps_ref[:, pl.ds(j * LANES, LANES)].astype(jnp.float32)

    def tap_kernel(t):
        both = taps_rows[pl.ds(t, half, stride=stride), :]
        return jnp.concatenate([both[:, :out_chan], both[:, out_chan:]], axis=0)

    group = LANES // in_chan
    for t in range(0, 27, group):
        some = jnp.concatenate([tap_kernel(t + k) for k in range(min(group, 27 - t))], axis=0)
        wf[:, pl.ds(t * in_chan, some.shape[0])] = some.T.astype(jnp.bfloat16)
    wb[...] = jnp.zeros_like(wb)
    for a in range(3):
        for t in range(0, 9, 2):
            some = [tap_kernel(26 - 9 * a - t - k) for k in range(min(2, 9 - t))]
            some = jnp.concatenate(some, axis=1).astype(jnp.bfloat16)
            for z in range(planes):
                at = pl.ds((z + a) * deep_u + t * out_chan, some.shape[1])
                wb[pl.ds(z * in_chan, in_chan), at] = some

    pad = deep_u - 9 * out_chan
    for vol in range(vols):
        if pad:
            for slot in range(planes + 2):
                at = pl.ds(slot * deep_u + 9 * out_chan, pad)
                near_u[vol, at, :] = jnp.zeros((pad, cells), jnp.bfloat16)
        for z in range(planes):
            for piece in range(out_chan // ROWS):
                fill(near_u, vol, (z + 1) * deep_u, out_chan, piece, piece_u(vol, z, piece))

    rows = (((1,), (0,)), ((), ()))
    bias = jnp.broadcast_to(bias_ref[...], (LANES, out_chan)).T
    bias = jnp.concatenate([bias] * (cells // LANES), axis=1)
    for vol in range(vols):
        for z in range(planes):
            window = near_x[vol, pl.ds(z * deep_x, 3 * deep_x), :]
            value = lax.dot_general(wf[...], window, rows, preferred_element_type=jnp.float32)
            put(rows_u, vol, pl.ds(z, out_chan, stride=planes), value + bias)
    for step in range(1, n_in):
        in_copy(step, 0).wait_recv()
        in_copy(step, 1).wait_recv()
    total_a, total_b = part_a[me_in], part_b[me_in]
    for step in range(1, n_in):
        total_a += recv_a[step - 1]
        total_b += recv_b[step - 1]
    acc[...] = jnp.concatenate([total_a, total_b], axis=0).reshape(acc.shape)
    for step in range(1, n_out):
        out_copy(step).start()

    for side in range(2):

        @pl.when(gets[side])
        def _(side=side):
            halo_copies(side, (1,))[0].wait_recv()

    for vol in range(vols):
        for side, slot in ((0, 0), (1, planes + 1)):
            for piece in range(out_chan // ROWS):
                field = halo_u[side, vol, pl.ds(piece * ROWS, ROWS), :].astype(jnp.float32)
                fill(near_u, vol, slot * deep_u, out_chan, piece, field)
    for vol in range(vols):
        unite(rows_u, vol, out_ref, out_chan)

    def backward(first):
        tile = min(2 * LANES, cells)
        for vol in range(vols):
            for at in range(0 if first else tile, tile if first else cells, tile):
                field = near_u[vol, :, pl.ds(at, tile)]
                value = lax.dot_general(wb[...], field, rows, preferred_element_type=jnp.float32)
                for z in range(planes):
                    for piece in range(2):
                        low = z * in_chan + piece * half
                        out = pl.ds(piece * planes + z, half, stride=2 * planes)
                        for k in range(tile // LANES):
                            part_k = value[low : low + half, k * LANES : (k + 1) * LANES]
                            rows_x[vol, at // LANES + k, out, :] = part_k

    for step in range(1, n_out):
        out_copy(step).wait_recv()
    total = acc[me_out]
    for step in range(1, n_out):
        total += recv_out[step - 1]
    gath[me_in, me_out] = (total * factor).astype(jnp.bfloat16)
    for step in range(1, n_out):
        gather_out_copy(step).start()
    backward(True)
    for step in range(1, n_out):
        gather_out_copy(step).wait_recv()
    for step in range(1, n_in):
        gather_in_copy(step).start()
    backward(False)
    for vol in range(vols):
        unite(rows_x, vol, gi_ref, in_chan)
    for step in range(1, n_in):
        gather_in_copy(step).wait_recv()
    size_a, size_b = part_a.shape[1], part_b.shape[1]
    for peer in range(n_in):
        value = gath[peer].astype(jnp.float32).reshape(size_a + size_b, LANES)
        sums_a[pl.ds(peer * size_a, size_a), :] = value[:size_a]
        sums_b[pl.ds(peer * size_b, size_b), :] = value[size_a:]
    for j in range(half):
        value = [
            sums_b[pl.ds(j, 9, stride=half), :],
            sums_a[pl.ds(j, 9, stride=half), :],
            sums_b[pl.ds(9 * half + j, 9, stride=half), :],
        ]
        wg_ref[:, pl.ds(j * LANES, LANES)] = jnp.concatenate(value, axis=0)
    bg_ref[...] = sums_a[pl.ds(9 * half, 1), :out_chan]

    for side in range(2):

        @pl.when(sends[side])
        def _(side=side):
            for copy in halo_copies(side):
                copy.wait_send()

    for step in range(1, n_in):
        in_copy(step, 0).wait_send()
        in_copy(step, 1).wait_send()
        gather_in_copy(step).wait_send()
    for step in range(1, n_out):
        out_copy(step).wait_send()
        gather_out_copy(step).wait_send()


def finish(*refs):
    sem = refs[8]
    copies = [pltpu.make_async_copy(refs[k], refs[4 + k], sem.at[k]) for k in range(4)]
    for copy in copies:
        copy.start()
    for copy in copies:
        copy.wait()


def on_device(sizes, features_in, kernel_taps, channel_bias, upstream):
    inner_dp, n_gz, n_in, n_out = sizes
    vols, in_chan, planes, cells = features_in.shape
    out_chan = upstream.shape[1]
    half = in_chan // 2
    cells_all = vols * inner_dp * n_out * planes * n_gz * cells
    factor = 1.0 / math.sqrt(cells_all)
    size_a = 8 * -(-(9 * half + 8) // (8 * n_in))
    size_b = 8 * -(-(18 * half) // (8 * n_in))
    per = ROWS * -(-(size_a + size_b) // (ROWS * n_out))
    size_b = n_out * per - size_a
    vmem = pl.BlockSpec(memory_space=pltpu.VMEM)
    hbm = pl.BlockSpec(memory_space=pltpu.HBM)
    dma = pltpu.SemaphoreType.DMA
    steps_in, steps_out = max(n_in - 1, 1), max(n_out - 1, 1)
    scratch = [
        pltpu.VMEM(features_in.shape, jnp.bfloat16),
        pltpu.VMEM(upstream.shape, jnp.bfloat16),
        pltpu.VMEM(kernel_taps.shape, jnp.bfloat16),
        pltpu.VMEM((1, out_chan), jnp.float32),
        dma((4,)),
        pltpu.VMEM((vols, planes * out_chan, cells), jnp.bfloat16),
        pltpu.VMEM((vols, cells // LANES, in_chan * planes, LANES), jnp.float32),
        pltpu.VMEM((vols, cells // LANES, out_chan * planes, LANES), jnp.float32),
        pltpu.VMEM((2, vols, in_chan, cells), jnp.bfloat16),
        pltpu.VMEM((2, vols, out_chan, cells), jnp.bfloat16),
        pltpu.VMEM((32 * half, LANES), jnp.float32),
        pltpu.VMEM((out_chan, 27 * in_chan), jnp.bfloat16),
        pltpu.VMEM((planes * in_chan, (planes + 2) * depth(out_chan)), jnp.bfloat16),
        pltpu.VMEM((2, vols, in_chan, cells), jnp.bfloat16),
        pltpu.VMEM((2, vols, out_chan, cells), jnp.bfloat16),
        pltpu.VMEM((vols, (planes + 2) * 9 * in_chan, cells), jnp.bfloat16),
        pltpu.VMEM((vols, (planes + 2) * depth(out_chan), cells), jnp.bfloat16),
        pltpu.VMEM((n_in, size_a, LANES), jnp.float32),
        pltpu.VMEM((n_in, size_b, LANES), jnp.float32),
        pltpu.VMEM((steps_in, size_a, LANES), jnp.float32),
        pltpu.VMEM((steps_in, size_b, LANES), jnp.float32),
        pltpu.VMEM((n_out, per, LANES), jnp.float32),
        pltpu.VMEM((steps_out, per, LANES), jnp.float32),
        pltpu.VMEM((n_in, n_out, per, LANES), jnp.bfloat16),
        pltpu.VMEM((n_in * size_a, LANES), jnp.float32),
        pltpu.VMEM((n_in * size_b, LANES), jnp.float32),
        dma((2, 2)),
        dma((2, 2)),
        dma((2, steps_in)),
        dma((2, steps_in)),
        dma((steps_out,)),
        dma((steps_out,)),
        dma((steps_out,)),
        dma((steps_out,)),
        dma((steps_in,)),
        dma((steps_in,)),
    ]
    held = [each for each in scratch if each.memory_space == pltpu.VMEM]
    grant = sum(math.prod(each.shape) * jnp.dtype(each.dtype).itemsize for each in held)
    results = pl.pallas_call(
        functools.partial(kernel, sizes, factor),
        out_shape=(
            jax.ShapeDtypeStruct(upstream.shape, jnp.bfloat16),
            jax.ShapeDtypeStruct(features_in.shape, jnp.bfloat16),
            jax.ShapeDtypeStruct(kernel_taps.shape, jnp.float32),
            jax.ShapeDtypeStruct((1, out_chan), jnp.float32),
        ),
        in_specs=[hbm] * 4,
        out_specs=(vmem,) * 4,
        scratch_shapes=scratch,
        compiler_params=pltpu.CompilerParams(
            collective_id=0, has_side_effects=True, vmem_limit_bytes=grant + 6 * 2**20
        ),
    )(
        pltpu.with_memory_space_constraint(features_in, pltpu.HBM),
        pltpu.with_memory_space_constraint(upstream, pltpu.HBM),
        pltpu.with_memory_space_constraint(kernel_taps, pltpu.HBM),
        pltpu.with_memory_space_constraint(channel_bias.reshape(1, out_chan), pltpu.HBM),
    )
    output, grad_input, weight_grad, bias_grad = pl.pallas_call(
        finish,
        out_shape=tuple(jax.ShapeDtypeStruct(each.shape, each.dtype) for each in results),
        in_specs=[vmem] * 4,
        out_specs=(hbm,) * 4,
        scratch_shapes=[dma((4,))],
        compiler_params=pltpu.CompilerParams(vmem_limit_bytes=4 * 2**20),
    )(*results)
    return (output, grad_input, weight_grad, bias_grad.reshape(out_chan))


def solution(mesh):
    n_dp, n_gz = mesh.shape["dp"], mesh.shape["gz"]
    inner_dp = max(d for d in range(1, n_dp + 1) if n_dp % d == 0 and d * d <= n_dp)
    sizes = (inner_dp, n_gz, inner_dp * n_gz, n_dp // inner_dp)
    in_specs = (P("dp", None, "gz", None), P(), P(), P("dp", None, "gz", None))
    out_specs = (P("dp", None, "gz", None), P("dp", None, "gz", None), P(), P())
    return jax.shard_map(
        functools.partial(on_device, sizes),
        mesh=mesh,
        in_specs=in_specs,
        out_specs=out_specs,
        check_vma=False,
    )
```

```python
import functools
import math

import jax
import jax.numpy as jnp
from jax import lax
from jax.experimental import pallas as pl
from jax.experimental.pallas import tpu as pltpu
from jax.sharding import PartitionSpec as P

NX = 64
NY = 8
MESH = pl.DeviceIdType.MESH
LANES = 128
ROWS = 16


def shifted(field):
    cells = field.shape[1]
    at = lax.broadcasted_iota(jnp.int32, field.shape, 1)
    col = at % NX
    zero = jnp.zeros_like(field)
    sides = (
        jnp.where(col == 0, zero, pltpu.roll(field, 1, 1)),
        field,
        jnp.where(col == NX - 1, zero, pltpu.roll(field, cells - 1, 1)),
    )
    found = [jnp.where(at < NX, zero, pltpu.roll(side, NX, 1)) for side in sides]
    found += list(sides)
    found += [jnp.where(at >= cells - NX, zero, pltpu.roll(side, cells - NX, 1)) for side in sides]
    return [each.astype(jnp.bfloat16) for each in found]


def fill(buf, vol, start, chan, piece, field):
    for tap, value in enumerate(shifted(field)):
        buf[vol, pl.ds(start + tap * chan + piece * ROWS, ROWS), :] = value


def depth(chan):
    return LANES * -(-9 * chan // LANES)


def kernel(
    sizes, factor, x_hbm, u_hbm, taps_hbm, bias_hbm, out_ref, gi_ref, wg_ref, bg_ref,
    x_ref, u_ref, taps_ref, bias_ref, load, grads, rows_x, rows_u, edge_x, edge_u, taps_rows, wf, wb,
    halo_x, halo_u, near_x, near_u, part_a, part_b, recv_a, recv_b, acc, recv_out, gath,
    sums_a, sums_b,
    halo_send, halo_recv, in_send, in_recv, out_send, out_recv,
    gout_send, gout_recv, gin_send, gin_recv,
):
    inner_dp, n_gz, n_in, n_out = sizes
    vols, in_chan, planes, cells = x_ref.shape
    out_chan = u_ref.shape[1]
    half = in_chan // 2
    dp, gz = lax.axis_index("dp"), lax.axis_index("gz")
    me_in = lax.rem(dp, inner_dp) * n_gz + gz
    me_out = lax.div(dp, inner_dp)

    @functools.cache
    def inner_peer(step):
        peer = lax.rem(me_in + step, n_in)
        return peer, {"dp": me_out * inner_dp + lax.div(peer, n_gz), "gz": lax.rem(peer, n_gz)}

    @functools.cache
    def outer_peer(step):
        peer = lax.rem(me_out + step, n_out)
        return peer, {"dp": peer * inner_dp + lax.rem(dp, inner_dp), "gz": gz}

    tiles = cells // LANES

    def piece_x(vol, z, piece):
        at = pl.ds(piece * planes + z, half, stride=2 * planes)
        return jnp.concatenate([rows_x[vol, tile, at, :] for tile in range(tiles)], axis=1)

    def piece_u(vol, z, piece):
        at = pl.ds(piece * ROWS * planes + z, ROWS, stride=planes)
        return jnp.concatenate([rows_u[vol, tile, at, :] for tile in range(tiles)], axis=1)

    def spread(rows, vol, ref, chan):
        for i in range(chan):
            value = ref[vol, i].astype(jnp.float32)
            for tile in range(tiles):
                at = slice(tile * LANES, (tile + 1) * LANES)
                rows[vol, tile, pl.ds(i * planes, planes), :] = value[:, at]

    def put(rows, vol, at, value):
        for tile in range(tiles):
            rows[vol, tile, at, :] = value[:, tile * LANES : (tile + 1) * LANES]

    def unite(rows, vol, ref, chan):
        for i in range(chan):
            at = pl.ds(i * planes, planes)
            value = jnp.concatenate([rows[vol, tile, at, :] for tile in range(tiles)], axis=1)
            ref[vol, i] = value.astype(jnp.bfloat16)

    moves = ((x_hbm, x_ref), (u_hbm, u_ref), (taps_hbm, taps_ref), (bias_hbm, bias_ref))
    loads = [
        pltpu.make_async_copy(source, target, load.at[at])
        for at, (source, target) in enumerate(moves)
    ]
    for copy in loads:
        copy.start()
    barrier = pltpu.get_barrier_semaphore()
    for step in range(1, n_in):
        pl.semaphore_signal(barrier, inc=1, device_id=inner_peer(step)[1], device_id_type=MESH)
    for step in range(1, n_out):
        pl.semaphore_signal(barrier, inc=1, device_id=outer_peer(step)[1], device_id_type=MESH)

    deep_x, deep_u = 9 * in_chan, depth(out_chan)
    pad = deep_u - 9 * out_chan
    wb[...] = jnp.zeros_like(wb)
    for vol in range(vols):
        if pad:
            for slot in range(planes + 2):
                at = pl.ds(slot * deep_u + 9 * out_chan, pad)
                near_u[vol, at, :] = jnp.zeros((pad, cells), jnp.bfloat16)
    loads[0].wait()
    for vol in range(vols):
        spread(rows_x, vol, x_ref, in_chan)
        for side, z in ((0, planes - 1), (1, 0)):
            for piece in range(2):
                at = pl.ds(piece * half, half)
                edge_x[side, vol, at, :] = piece_x(vol, z, piece).astype(jnp.bfloat16)

    pl.semaphore_wait(barrier, n_in + n_out - 2)

    def halo_copies(side, which=(0, 1)):
        target = gz + 1 if side == 0 else gz - 1
        return [
            pltpu.make_async_remote_copy(
                src_ref=ref.at[side],
                dst_ref=halo.at[side],
                send_sem=halo_send.at[side, at],
                recv_sem=halo_recv.at[side, at],
                device_id={"gz": target},
                device_id_type=MESH,
            )
            for at, (ref, halo) in enumerate(((edge_x, halo_x), (edge_u, halo_u)))
            if at in which
        ]

    sends = (gz < n_gz - 1, gz > 0)
    gets = (gz > 0, gz < n_gz - 1)
    def send_halos(which):
        for side in range(2):

            @pl.when(sends[side])
            def _(side=side):
                halo_copies(side, (which,))[0].start()

    send_halos(0)
    loads[1].wait()
    for vol in range(vols):
        spread(rows_u, vol, u_ref, out_chan)
        for z in range(planes):
            for piece in range(out_chan // ROWS):
                value = piece_u(vol, z, piece).astype(jnp.bfloat16)
                grads[vol, pl.ds(z * out_chan + piece * ROWS, ROWS), :] = value
        for side, z in ((0, planes - 1), (1, 0)):
            edge_u[side, vol] = grads[vol, pl.ds(z * out_chan, out_chan), :]
    send_halos(1)
    lanes = (((1,), (1,)), ((), ()))
    for vol in range(vols):
        for z in range(planes):
            for piece in range(2):
                fill(near_x, vol, (z + 1) * deep_x, in_chan, piece, piece_x(vol, z, piece))

    def product(vol, slot, count, at, wide):
        window = near_x[vol, pl.ds(slot * deep_x, count * deep_x), :]
        grad = grads[vol, pl.ds(at, wide), :]
        return lax.dot_general(window, grad, lanes, preferred_element_type=jnp.float32)

    def lane_tile(value, k):
        return value[:, k * LANES : (k + 1) * LANES]

    last = planes * out_chan - LANES
    even = [jnp.zeros((deep_x, LANES), jnp.float32) for _ in range(3)]
    odd = [jnp.zeros((deep_x, LANES), jnp.float32) for _ in range(3)]
    ones = jnp.ones((8, cells), jnp.bfloat16)
    bias_term = jnp.zeros((8, LANES), jnp.float32)
    for vol in range(vols):
        inside = product(vol, 1, planes, 0, planes * out_chan)
        for tap in range(3):
            for z in range(planes):
                if 1 <= z + tap <= planes:
                    low = (z + tap - 1) * deep_x
                    kept = odd if z % 2 else even
                    kept[tap] += lane_tile(inside[low : low + deep_x], z // 2)
        bias_all = lax.dot_general(
            ones, grads[vol], lanes, preferred_element_type=jnp.float32
        )
        for k in range(planes // 2):
            bias_term += lane_tile(bias_all, k)

    def packed(tap):
        first = even[tap].reshape(9, 2, half, LANES)
        second = odd[tap].reshape(9, 2, half, LANES)
        low = lax.broadcasted_iota(jnp.int32, (9, half, LANES), 2) < out_chan
        stay = jnp.where(low, first[:, 0], second[:, 1]).reshape(9 * half, LANES)
        move = jnp.where(low, first[:, 1], second[:, 0]).reshape(9 * half, LANES)
        return stay + pltpu.roll(move, out_chan, 1)

    def lay(part, pieces):
        rest = math.prod(part.shape[:2]) - sum(each.shape[0] for each in pieces)
        if rest:
            pieces = pieces + [jnp.zeros((rest, LANES), jnp.float32)]
        part[...] = jnp.concatenate(pieces, axis=0).reshape(part.shape)

    def in_copy(step, second):
        peer, device = inner_peer(step)
        return pltpu.make_async_remote_copy(
            src_ref=(part_b if second else part_a).at[peer],
            dst_ref=(recv_b if second else recv_a).at[step - 1],
            send_sem=in_send.at[second, step - 1],
            recv_sem=in_recv.at[second, step - 1],
            device_id=device,
            device_id_type=MESH,
        )

    bias_term += pltpu.roll(bias_term, out_chan, 1)
    lay(part_a, [packed(1), bias_term])
    for step in range(1, n_in):
        in_copy(step, 0).start()

    for side in range(2):

        @pl.when(gets[side])
        def _(side=side):
            halo_copies(side, (0,))[0].wait_recv()

        @pl.when(jnp.logical_not(gets[side]))
        def _(side=side):
            halo_x[side] = jnp.zeros(halo_x.shape[1:], halo_x.dtype)
            halo_u[side] = jnp.zeros(halo_u.shape[1:], halo_u.dtype)

    for vol in range(vols):
        for side, slot in ((0, 0), (1, planes + 1)):
            for piece in range(2):
                field = halo_x[side, vol, pl.ds(piece * half, half), :].astype(jnp.float32)
                fill(near_x, vol, slot * deep_x, in_chan, piece, field)
        even[0] += product(vol, 0, 1, 0, LANES)
        odd[2] += product(vol, planes + 1, 1, last, LANES)
    lay(part_b, [packed(0), packed(2)])
    for step in range(1, n_in):
        in_copy(step, 1).start()

    def out_copy(step):
        peer, device = outer_peer(step)
        return pltpu.make_async_remote_copy(
            src_ref=acc.at[peer],
            dst_ref=recv_out.at[step - 1],
            send_sem=out_send.at[step - 1],
            recv_sem=out_recv.at[step - 1],
            device_id=device,
            device_id_type=MESH,
        )

    def gather_out_copy(step):
        return pltpu.make_async_remote_copy(
            src_ref=gath.at[me_in, me_out],
            dst_ref=gath.at[me_in, me_out],
            send_sem=gout_send.at[step - 1],
            recv_sem=gout_recv.at[step - 1],
            device_id=outer_peer(step)[1],
            device_id_type=MESH,
        )

    def gather_in_copy(step):
        return pltpu.make_async_remote_copy(
            src_ref=gath.at[me_in],
            dst_ref=gath.at[me_in],
            send_sem=gin_send.at[step - 1],
            recv_sem=gin_recv.at[step - 1],
            device_id=inner_peer(step)[1],
            device_id_type=MESH,
        )

    loads[2].wait()
    loads[3].wait()
    stride = taps_rows.shape[0] // half
    for j in range(half):
        taps_rows[pl.ds(j * stride, 27), :] = taps_ref[:, pl.ds(j * LANES, LANES)].astype(jnp.float32)

    def tap_kernel(t):
        both = taps_rows[pl.ds(t, half, stride=stride), :]
        return jnp.concatenate([both[:, :out_chan], both[:, out_chan:]], axis=0)

    group = LANES // in_chan
    for t in range(0, 27, group):
        some = jnp.concatenate([tap_kernel(t + k) for k in range(min(group, 27 - t))], axis=0)
        wf[:, pl.ds(t * in_chan, some.shape[0])] = some.T.astype(jnp.bfloat16)
    for a in range(3):
        for t in range(0, 9, 2):
            some = [tap_kernel(26 - 9 * a - t - k) for k in range(min(2, 9 - t))]
            some = jnp.concatenate(some, axis=1).astype(jnp.bfloat16)
            for z in range(planes):
                at = pl.ds((z + a) * deep_u + t * out_chan, some.shape[1])
                wb[pl.ds(z * in_chan, in_chan), at] = some

    for vol in range(vols):
        for z in range(planes):
            for piece in range(out_chan // ROWS):
                fill(near_u, vol, (z + 1) * deep_u, out_chan, piece, piece_u(vol, z, piece))

    rows = (((1,), (0,)), ((), ()))
    for step in range(1, n_in):
        in_copy(step, 0).wait_recv()
        in_copy(step, 1).wait_recv()
    total_a, total_b = part_a[me_in], part_b[me_in]
    for step in range(1, n_in):
        total_a += recv_a[step - 1]
        total_b += recv_b[step - 1]
    acc[...] = jnp.concatenate([total_a, total_b], axis=0).reshape(acc.shape)
    for step in range(1, n_out):
        out_copy(step).start()

    bias = jnp.broadcast_to(bias_ref[...], (LANES, out_chan)).T
    bias = jnp.concatenate([bias] * (cells // LANES), axis=1)
    for vol in range(vols):
        for z in range(planes):
            window = near_x[vol, pl.ds(z * deep_x, 3 * deep_x), :]
            value = lax.dot_general(wf[...], window, rows, preferred_element_type=jnp.float32)
            put(rows_u, vol, pl.ds(z, out_chan, stride=planes), value + bias)
    def backward(first):
        tile = min(2 * LANES, cells)
        for vol in range(vols):
            for at in range(0 if first else tile, tile if first else cells, tile):
                field = near_u[vol, :, pl.ds(at, tile)]
                value = lax.dot_general(wb[...], field, rows, preferred_element_type=jnp.float32)
                for z in range(planes):
                    for piece in range(2):
                        low = z * in_chan + piece * half
                        out = pl.ds(piece * planes + z, half, stride=2 * planes)
                        for k in range(tile // LANES):
                            part_k = value[low : low + half, k * LANES : (k + 1) * LANES]
                            rows_x[vol, at // LANES + k, out, :] = part_k

    for step in range(1, n_out):
        out_copy(step).wait_recv()
    total = acc[me_out]
    for step in range(1, n_out):
        total += recv_out[step - 1]
    gath[me_in, me_out] = (total * factor).astype(jnp.bfloat16)
    for step in range(1, n_out):
        gather_out_copy(step).start()
    for side in range(2):

        @pl.when(gets[side])
        def _(side=side):
            halo_copies(side, (1,))[0].wait_recv()

    for vol in range(vols):
        for side, slot in ((0, 0), (1, planes + 1)):
            for piece in range(out_chan // ROWS):
                field = halo_u[side, vol, pl.ds(piece * ROWS, ROWS), :].astype(jnp.float32)
                fill(near_u, vol, slot * deep_u, out_chan, piece, field)
    backward(True)
    for step in range(1, n_out):
        gather_out_copy(step).wait_recv()
    for step in range(1, n_in):
        gather_in_copy(step).start()
    for vol in range(vols):
        unite(rows_u, vol, out_ref, out_chan)
    backward(False)
    for vol in range(vols):
        unite(rows_x, vol, gi_ref, in_chan)
    for step in range(1, n_in):
        gather_in_copy(step).wait_recv()
    size_a, size_b = part_a.shape[1], part_b.shape[1]
    for peer in range(n_in):
        value = gath[peer].astype(jnp.float32).reshape(size_a + size_b, LANES)
        sums_a[pl.ds(peer * size_a, size_a), :] = value[:size_a]
        sums_b[pl.ds(peer * size_b, size_b), :] = value[size_a:]
    for j in range(half):
        value = [
            sums_b[pl.ds(j, 9, stride=half), :],
            sums_a[pl.ds(j, 9, stride=half), :],
            sums_b[pl.ds(9 * half + j, 9, stride=half), :],
        ]
        wg_ref[:, pl.ds(j * LANES, LANES)] = jnp.concatenate(value, axis=0)
    bg_ref[...] = sums_a[pl.ds(9 * half, 1), :out_chan]

    for side in range(2):

        @pl.when(sends[side])
        def _(side=side):
            for copy in halo_copies(side):
                copy.wait_send()

    for step in range(1, n_in):
        in_copy(step, 0).wait_send()
        in_copy(step, 1).wait_send()
        gather_in_copy(step).wait_send()
    for step in range(1, n_out):
        out_copy(step).wait_send()
        gather_out_copy(step).wait_send()


def finish(*refs):
    sem = refs[8]
    copies = [pltpu.make_async_copy(refs[k], refs[4 + k], sem.at[k]) for k in range(4)]
    for copy in copies:
        copy.start()
    for copy in copies:
        copy.wait()


def on_device(sizes, features_in, kernel_taps, channel_bias, upstream):
    inner_dp, n_gz, n_in, n_out = sizes
    vols, in_chan, planes, cells = features_in.shape
    out_chan = upstream.shape[1]
    half = in_chan // 2
    cells_all = vols * inner_dp * n_out * planes * n_gz * cells
    factor = 1.0 / math.sqrt(cells_all)
    size_a = 8 * -(-(9 * half + 8) // (8 * n_in))
    size_b = 8 * -(-(18 * half) // (8 * n_in))
    per = ROWS * -(-(size_a + size_b) // (ROWS * n_out))
    size_b = n_out * per - size_a
    vmem = pl.BlockSpec(memory_space=pltpu.VMEM)
    hbm = pl.BlockSpec(memory_space=pltpu.HBM)
    dma = pltpu.SemaphoreType.DMA
    steps_in, steps_out = max(n_in - 1, 1), max(n_out - 1, 1)
    scratch = [
        pltpu.VMEM(features_in.shape, jnp.bfloat16),
        pltpu.VMEM(upstream.shape, jnp.bfloat16),
        pltpu.VMEM(kernel_taps.shape, jnp.bfloat16),
        pltpu.VMEM((1, out_chan), jnp.float32),
        dma((4,)),
        pltpu.VMEM((vols, planes * out_chan, cells), jnp.bfloat16),
        pltpu.VMEM((vols, cells // LANES, in_chan * planes, LANES), jnp.float32),
        pltpu.VMEM((vols, cells // LANES, out_chan * planes, LANES), jnp.float32),
        pltpu.VMEM((2, vols, in_chan, cells), jnp.bfloat16),
        pltpu.VMEM((2, vols, out_chan, cells), jnp.bfloat16),
        pltpu.VMEM((32 * half, LANES), jnp.float32),
        pltpu.VMEM((out_chan, 27 * in_chan), jnp.bfloat16),
        pltpu.VMEM((planes * in_chan, (planes + 2) * depth(out_chan)), jnp.bfloat16),
        pltpu.VMEM((2, vols, in_chan, cells), jnp.bfloat16),
        pltpu.VMEM((2, vols, out_chan, cells), jnp.bfloat16),
        pltpu.VMEM((vols, (planes + 2) * 9 * in_chan, cells), jnp.bfloat16),
        pltpu.VMEM((vols, (planes + 2) * depth(out_chan), cells), jnp.bfloat16),
        pltpu.VMEM((n_in, size_a, LANES), jnp.float32),
        pltpu.VMEM((n_in, size_b, LANES), jnp.float32),
        pltpu.VMEM((steps_in, size_a, LANES), jnp.float32),
        pltpu.VMEM((steps_in, size_b, LANES), jnp.float32),
        pltpu.VMEM((n_out, per, LANES), jnp.float32),
        pltpu.VMEM((steps_out, per, LANES), jnp.float32),
        pltpu.VMEM((n_in, n_out, per, LANES), jnp.bfloat16),
        pltpu.VMEM((n_in * size_a, LANES), jnp.float32),
        pltpu.VMEM((n_in * size_b, LANES), jnp.float32),
        dma((2, 2)),
        dma((2, 2)),
        dma((2, steps_in)),
        dma((2, steps_in)),
        dma((steps_out,)),
        dma((steps_out,)),
        dma((steps_out,)),
        dma((steps_out,)),
        dma((steps_in,)),
        dma((steps_in,)),
    ]
    held = [each for each in scratch if each.memory_space == pltpu.VMEM]
    grant = sum(math.prod(each.shape) * jnp.dtype(each.dtype).itemsize for each in held)
    results = pl.pallas_call(
        functools.partial(kernel, sizes, factor),
        out_shape=(
            jax.ShapeDtypeStruct(upstream.shape, jnp.bfloat16),
            jax.ShapeDtypeStruct(features_in.shape, jnp.bfloat16),
            jax.ShapeDtypeStruct(kernel_taps.shape, jnp.float32),
            jax.ShapeDtypeStruct((1, out_chan), jnp.float32),
        ),
        in_specs=[hbm] * 4,
        out_specs=(vmem,) * 4,
        scratch_shapes=scratch,
        compiler_params=pltpu.CompilerParams(
            collective_id=0, has_side_effects=True, vmem_limit_bytes=grant + 6 * 2**20
        ),
    )(
        pltpu.with_memory_space_constraint(features_in, pltpu.HBM),
        pltpu.with_memory_space_constraint(upstream, pltpu.HBM),
        pltpu.with_memory_space_constraint(kernel_taps, pltpu.HBM),
        pltpu.with_memory_space_constraint(channel_bias.reshape(1, out_chan), pltpu.HBM),
    )
    output, grad_input, weight_grad, bias_grad = pl.pallas_call(
        finish,
        out_shape=tuple(jax.ShapeDtypeStruct(each.shape, each.dtype) for each in results),
        in_specs=[vmem] * 4,
        out_specs=(hbm,) * 4,
        scratch_shapes=[dma((4,))],
        compiler_params=pltpu.CompilerParams(vmem_limit_bytes=4 * 2**20),
    )(*results)
    return (output, grad_input, weight_grad, bias_grad.reshape(out_chan))


def solution(mesh):
    n_dp, n_gz = mesh.shape["dp"], mesh.shape["gz"]
    inner_dp = max(d for d in range(1, n_dp + 1) if n_dp % d == 0 and d * d <= n_dp)
    sizes = (inner_dp, n_gz, inner_dp * n_gz, n_dp // inner_dp)
    in_specs = (P("dp", None, "gz", None), P(), P(), P("dp", None, "gz", None))
    out_specs = (P("dp", None, "gz", None), P("dp", None, "gz", None), P(), P())
    return jax.shard_map(
        functools.partial(on_device, sizes),
        mesh=mesh,
        in_specs=in_specs,
        out_specs=out_specs,
        check_vma=False,
    )
```

```python
import functools
import math

import jax
import jax.numpy as jnp
from jax import lax
from jax.experimental import pallas as pl
from jax.experimental.pallas import tpu as pltpu
from jax.sharding import PartitionSpec as P

NX = 64
NY = 8
MESH = pl.DeviceIdType.MESH
LANES = 128
ROWS = 16


def shifted(field):
    cells = field.shape[1]
    at = lax.broadcasted_iota(jnp.int32, field.shape, 1)
    col = at % NX
    zero = jnp.zeros_like(field)
    sides = (
        jnp.where(col == 0, zero, pltpu.roll(field, 1, 1)),
        field,
        jnp.where(col == NX - 1, zero, pltpu.roll(field, cells - 1, 1)),
    )
    found = [jnp.where(at < NX, zero, pltpu.roll(side, NX, 1)) for side in sides]
    found += list(sides)
    found += [jnp.where(at >= cells - NX, zero, pltpu.roll(side, cells - NX, 1)) for side in sides]
    return [each.astype(jnp.bfloat16) for each in found]


def fill(buf, vol, start, chan, piece, field):
    for tap, value in enumerate(shifted(field)):
        buf[vol, pl.ds(start + tap * chan + piece * ROWS, ROWS), :] = value


def depth(chan):
    return LANES * -(-9 * chan // LANES)


def kernel(
    sizes, factor, x_hbm, u_hbm, taps_hbm, bias_hbm, out_ref, gi_ref, wg_ref, bg_ref,
    x_ref, u_ref, taps_ref, bias_ref, load, grads, rows_x, rows_u, edge_x, edge_u, taps_rows, wf, wb,
    halo_x, halo_u, near_x, near_u, part_a, part_b, recv_a, recv_b, acc, recv_out, gath,
    sums_a, sums_b,
    halo_send, halo_recv, in_send, in_recv, out_send, out_recv,
    gout_send, gout_recv, gin_send, gin_recv,
):
    inner_dp, n_gz, n_in, n_out = sizes
    vols, in_chan, planes, cells = x_ref.shape
    out_chan = u_ref.shape[1]
    half = in_chan // 2
    dp, gz = lax.axis_index("dp"), lax.axis_index("gz")
    me_in = lax.rem(dp, inner_dp) * n_gz + gz
    me_out = lax.div(dp, inner_dp)

    @functools.cache
    def inner_peer(step):
        peer = lax.rem(me_in + step, n_in)
        return peer, {"dp": me_out * inner_dp + lax.div(peer, n_gz), "gz": lax.rem(peer, n_gz)}

    @functools.cache
    def outer_peer(step):
        peer = lax.rem(me_out + step, n_out)
        return peer, {"dp": peer * inner_dp + lax.rem(dp, inner_dp), "gz": gz}

    tiles = cells // LANES

    def piece_x(vol, z, piece):
        at = pl.ds(piece * planes + z, half, stride=2 * planes)
        return jnp.concatenate([rows_x[vol, tile, at, :] for tile in range(tiles)], axis=1)

    def piece_u(vol, z, piece):
        at = pl.ds(piece * ROWS * planes + z, ROWS, stride=planes)
        return jnp.concatenate([rows_u[vol, tile, at, :] for tile in range(tiles)], axis=1)

    def spread(rows, vol, ref, chan):
        for i in range(chan):
            value = ref[vol, i].astype(jnp.float32)
            for tile in range(tiles):
                at = slice(tile * LANES, (tile + 1) * LANES)
                rows[vol, tile, pl.ds(i * planes, planes), :] = value[:, at]

    def put(rows, vol, at, value):
        for tile in range(tiles):
            rows[vol, tile, at, :] = value[:, tile * LANES : (tile + 1) * LANES]

    def unite(rows, vol, ref, chan):
        for i in range(chan):
            at = pl.ds(i * planes, planes)
            value = jnp.concatenate([rows[vol, tile, at, :] for tile in range(tiles)], axis=1)
            ref[vol, i] = value.astype(jnp.bfloat16)

    moves = ((x_hbm, x_ref), (u_hbm, u_ref), (taps_hbm, taps_ref), (bias_hbm, bias_ref))
    loads = [
        pltpu.make_async_copy(source, target, load.at[at])
        for at, (source, target) in enumerate(moves)
    ]
    for copy in loads:
        copy.start()
    barrier = pltpu.get_barrier_semaphore()
    for step in range(1, n_in):
        pl.semaphore_signal(barrier, inc=1, device_id=inner_peer(step)[1], device_id_type=MESH)
    for step in range(1, n_out):
        pl.semaphore_signal(barrier, inc=1, device_id=outer_peer(step)[1], device_id_type=MESH)

    deep_x, deep_u = depth(in_chan), depth(out_chan)
    wb[...] = jnp.zeros_like(wb)
    wf[...] = jnp.zeros_like(wf)
    for vol in range(vols):
        for near, deep, chan in ((near_x, deep_x, in_chan), (near_u, deep_u, out_chan)):
            pad = deep - 9 * chan
            if pad:
                for slot in range(planes + 2):
                    at = pl.ds(slot * deep + 9 * chan, pad)
                    near[vol, at, :] = jnp.zeros((pad, cells), jnp.bfloat16)
    loads[0].wait()
    for vol in range(vols):
        spread(rows_x, vol, x_ref, in_chan)
        for side, z in ((0, planes - 1), (1, 0)):
            for piece in range(2):
                at = pl.ds(piece * half, half)
                edge_x[side, vol, at, :] = piece_x(vol, z, piece).astype(jnp.bfloat16)

    pl.semaphore_wait(barrier, n_in + n_out - 2)

    def halo_copies(side, which=(0, 1)):
        target = gz + 1 if side == 0 else gz - 1
        return [
            pltpu.make_async_remote_copy(
                src_ref=ref.at[side],
                dst_ref=halo.at[side],
                send_sem=halo_send.at[side, at],
                recv_sem=halo_recv.at[side, at],
                device_id={"gz": target},
                device_id_type=MESH,
            )
            for at, (ref, halo) in enumerate(((edge_x, halo_x), (edge_u, halo_u)))
            if at in which
        ]

    sends = (gz < n_gz - 1, gz > 0)
    gets = (gz > 0, gz < n_gz - 1)
    def send_halos(which):
        for side in range(2):

            @pl.when(sends[side])
            def _(side=side):
                halo_copies(side, (which,))[0].start()

    send_halos(0)
    loads[1].wait()
    for vol in range(vols):
        spread(rows_u, vol, u_ref, out_chan)
        for z in range(planes):
            for piece in range(out_chan // ROWS):
                value = piece_u(vol, z, piece).astype(jnp.bfloat16)
                grads[vol, pl.ds(z * out_chan + piece * ROWS, ROWS), :] = value
        for side, z in ((0, planes - 1), (1, 0)):
            edge_u[side, vol] = grads[vol, pl.ds(z * out_chan, out_chan), :]
    send_halos(1)
    lanes = (((1,), (1,)), ((), ()))
    for vol in range(vols):
        for z in range(planes):
            for piece in range(2):
                fill(near_x, vol, (z + 1) * deep_x, in_chan, piece, piece_x(vol, z, piece))

    def product(vol, slot, at, wide):
        window = near_x[vol, pl.ds(slot * deep_x, 9 * in_chan), :]
        grad = grads[vol, pl.ds(at, wide), :]
        return lax.dot_general(window, grad, lanes, preferred_element_type=jnp.float32)

    def lane_tile(value, k):
        return value[:, k * LANES : (k + 1) * LANES]

    last = planes * out_chan - LANES
    even = [jnp.zeros((9 * in_chan, LANES), jnp.float32) for _ in range(3)]
    odd = [jnp.zeros((9 * in_chan, LANES), jnp.float32) for _ in range(3)]
    ones = jnp.ones((8, cells), jnp.bfloat16)
    bias_term = jnp.zeros((8, LANES), jnp.float32)
    for vol in range(vols):
        for slot in range(1, planes + 1):
            inside = product(vol, slot, 0, planes * out_chan)
            for tap in range(3):
                z = slot - tap
                if 0 <= z < planes:
                    kept = odd if z % 2 else even
                    kept[tap] += lane_tile(inside, z // 2)
        bias_all = lax.dot_general(
            ones, grads[vol], lanes, preferred_element_type=jnp.float32
        )
        for k in range(planes // 2):
            bias_term += lane_tile(bias_all, k)

    def packed(tap):
        first = even[tap].reshape(9, 2, half, LANES)
        second = odd[tap].reshape(9, 2, half, LANES)
        low = lax.broadcasted_iota(jnp.int32, (9, half, LANES), 2) < out_chan
        stay = jnp.where(low, first[:, 0], second[:, 1]).reshape(9 * half, LANES)
        move = jnp.where(low, first[:, 1], second[:, 0]).reshape(9 * half, LANES)
        return stay + pltpu.roll(move, out_chan, 1)

    def lay(part, pieces):
        rest = math.prod(part.shape[:2]) - sum(each.shape[0] for each in pieces)
        if rest:
            pieces = pieces + [jnp.zeros((rest, LANES), jnp.float32)]
        part[...] = jnp.concatenate(pieces, axis=0).reshape(part.shape)

    def in_copy(step, second):
        peer, device = inner_peer(step)
        return pltpu.make_async_remote_copy(
            src_ref=(part_b if second else part_a).at[peer],
            dst_ref=(recv_b if second else recv_a).at[step - 1],
            send_sem=in_send.at[second, step - 1],
            recv_sem=in_recv.at[second, step - 1],
            device_id=device,
            device_id_type=MESH,
        )

    bias_term += pltpu.roll(bias_term, out_chan, 1)
    lay(part_a, [packed(1), bias_term])
    for step in range(1, n_in):
        in_copy(step, 0).start()

    for side in range(2):

        @pl.when(gets[side])
        def _(side=side):
            halo_copies(side, (0,))[0].wait_recv()

        @pl.when(jnp.logical_not(gets[side]))
        def _(side=side):
            halo_x[side] = jnp.zeros(halo_x.shape[1:], halo_x.dtype)
            halo_u[side] = jnp.zeros(halo_u.shape[1:], halo_u.dtype)

    for vol in range(vols):
        for side, slot in ((0, 0), (1, planes + 1)):
            for piece in range(2):
                field = halo_x[side, vol, pl.ds(piece * half, half), :].astype(jnp.float32)
                fill(near_x, vol, slot * deep_x, in_chan, piece, field)
        even[0] += product(vol, 0, 0, LANES)
        odd[2] += product(vol, planes + 1, last, LANES)
    lay(part_b, [packed(0), packed(2)])
    for step in range(1, n_in):
        in_copy(step, 1).start()

    def out_copy(step):
        peer, device = outer_peer(step)
        return pltpu.make_async_remote_copy(
            src_ref=acc.at[peer],
            dst_ref=recv_out.at[step - 1],
            send_sem=out_send.at[step - 1],
            recv_sem=out_recv.at[step - 1],
            device_id=device,
            device_id_type=MESH,
        )

    def gather_out_copy(step):
        return pltpu.make_async_remote_copy(
            src_ref=gath.at[me_in, me_out],
            dst_ref=gath.at[me_in, me_out],
            send_sem=gout_send.at[step - 1],
            recv_sem=gout_recv.at[step - 1],
            device_id=outer_peer(step)[1],
            device_id_type=MESH,
        )

    def gather_in_copy(step):
        return pltpu.make_async_remote_copy(
            src_ref=gath.at[me_in],
            dst_ref=gath.at[me_in],
            send_sem=gin_send.at[step - 1],
            recv_sem=gin_recv.at[step - 1],
            device_id=inner_peer(step)[1],
            device_id_type=MESH,
        )

    loads[2].wait()
    loads[3].wait()
    stride = taps_rows.shape[0] // half
    for j in range(half):
        taps_rows[pl.ds(j * stride, 27), :] = taps_ref[:, pl.ds(j * LANES, LANES)].astype(jnp.float32)

    def tap_kernel(t):
        both = taps_rows[pl.ds(t, half, stride=stride), :]
        return jnp.concatenate([both[:, :out_chan], both[:, out_chan:]], axis=0)

    group = LANES // in_chan
    for a in range(3):
        for t in range(0, 9, group):
            some = [tap_kernel(9 * a + t + k) for k in range(min(group, 9 - t))]
            some = jnp.concatenate(some, axis=0).T.astype(jnp.bfloat16)
            for z in range(planes):
                at = pl.ds((z + a) * deep_x + t * in_chan, some.shape[1])
                wf[pl.ds(z * out_chan, out_chan), at] = some
    for a in range(3):
        for t in range(0, 9, 2):
            some = [tap_kernel(26 - 9 * a - t - k) for k in range(min(2, 9 - t))]
            some = jnp.concatenate(some, axis=1).astype(jnp.bfloat16)
            for z in range(planes):
                at = pl.ds((z + a) * deep_u + t * out_chan, some.shape[1])
                wb[pl.ds(z * in_chan, in_chan), at] = some

    for vol in range(vols):
        for z in range(planes):
            for piece in range(out_chan // ROWS):
                fill(near_u, vol, (z + 1) * deep_u, out_chan, piece, piece_u(vol, z, piece))

    rows = (((1,), (0,)), ((), ()))
    for step in range(1, n_in):
        in_copy(step, 0).wait_recv()
        in_copy(step, 1).wait_recv()
    total_a, total_b = part_a[me_in], part_b[me_in]
    for step in range(1, n_in):
        total_a += recv_a[step - 1]
        total_b += recv_b[step - 1]
    acc[...] = jnp.concatenate([total_a, total_b], axis=0).reshape(acc.shape)
    for step in range(1, n_out):
        out_copy(step).start()

    bias = jnp.broadcast_to(bias_ref[...], (LANES, out_chan)).T
    bias = jnp.concatenate([bias] * (cells // LANES), axis=1)
    for vol in range(vols):
        value = lax.dot_general(wf[...], near_x[vol], rows, preferred_element_type=jnp.float32)
        for z in range(planes):
            plane = value[z * out_chan : (z + 1) * out_chan]
            put(rows_u, vol, pl.ds(z, out_chan, stride=planes), plane + bias)

    def backward(first):
        tile = min(2 * LANES, cells)
        for vol in range(vols):
            for at in range(0 if first else tile, tile if first else cells, tile):
                field = near_u[vol, :, pl.ds(at, tile)]
                value = lax.dot_general(wb[...], field, rows, preferred_element_type=jnp.float32)
                for z in range(planes):
                    for piece in range(2):
                        low = z * in_chan + piece * half
                        out = pl.ds(piece * planes + z, half, stride=2 * planes)
                        for k in range(tile // LANES):
                            part_k = value[low : low + half, k * LANES : (k + 1) * LANES]
                            rows_x[vol, at // LANES + k, out, :] = part_k

    for step in range(1, n_out):
        out_copy(step).wait_recv()
    total = acc[me_out]
    for step in range(1, n_out):
        total += recv_out[step - 1]
    gath[me_in, me_out] = (total * factor).astype(jnp.bfloat16)
    for step in range(1, n_out):
        gather_out_copy(step).start()
    for side in range(2):

        @pl.when(gets[side])
        def _(side=side):
            halo_copies(side, (1,))[0].wait_recv()

    for vol in range(vols):
        for side, slot in ((0, 0), (1, planes + 1)):
            for piece in range(out_chan // ROWS):
                field = halo_u[side, vol, pl.ds(piece * ROWS, ROWS), :].astype(jnp.float32)
                fill(near_u, vol, slot * deep_u, out_chan, piece, field)
    backward(True)
    for step in range(1, n_out):
        gather_out_copy(step).wait_recv()
    for step in range(1, n_in):
        gather_in_copy(step).start()
    for vol in range(vols):
        unite(rows_u, vol, out_ref, out_chan)
    backward(False)
    for vol in range(vols):
        unite(rows_x, vol, gi_ref, in_chan)
    for step in range(1, n_in):
        gather_in_copy(step).wait_recv()
    size_a, size_b = part_a.shape[1], part_b.shape[1]
    for peer in range(n_in):
        value = gath[peer].astype(jnp.float32).reshape(size_a + size_b, LANES)
        sums_a[pl.ds(peer * size_a, size_a), :] = value[:size_a]
        sums_b[pl.ds(peer * size_b, size_b), :] = value[size_a:]
    for j in range(half):
        value = [
            sums_b[pl.ds(j, 9, stride=half), :],
            sums_a[pl.ds(j, 9, stride=half), :],
            sums_b[pl.ds(9 * half + j, 9, stride=half), :],
        ]
        wg_ref[:, pl.ds(j * LANES, LANES)] = jnp.concatenate(value, axis=0)
    bg_ref[...] = sums_a[pl.ds(9 * half, 1), :out_chan]

    for side in range(2):

        @pl.when(sends[side])
        def _(side=side):
            for copy in halo_copies(side):
                copy.wait_send()

    for step in range(1, n_in):
        in_copy(step, 0).wait_send()
        in_copy(step, 1).wait_send()
        gather_in_copy(step).wait_send()
    for step in range(1, n_out):
        out_copy(step).wait_send()
        gather_out_copy(step).wait_send()


def finish(*refs):
    sem = refs[8]
    copies = [pltpu.make_async_copy(refs[k], refs[4 + k], sem.at[k]) for k in range(4)]
    for copy in copies:
        copy.start()
    for copy in copies:
        copy.wait()


def on_device(sizes, features_in, kernel_taps, channel_bias, upstream):
    inner_dp, n_gz, n_in, n_out = sizes
    vols, in_chan, planes, cells = features_in.shape
    out_chan = upstream.shape[1]
    half = in_chan // 2
    cells_all = vols * inner_dp * n_out * planes * n_gz * cells
    factor = 1.0 / math.sqrt(cells_all)
    size_a = 8 * -(-(9 * half + 8) // (8 * n_in))
    size_b = 8 * -(-(18 * half) // (8 * n_in))
    per = ROWS * -(-(size_a + size_b) // (ROWS * n_out))
    size_b = n_out * per - size_a
    vmem = pl.BlockSpec(memory_space=pltpu.VMEM)
    hbm = pl.BlockSpec(memory_space=pltpu.HBM)
    dma = pltpu.SemaphoreType.DMA
    steps_in, steps_out = max(n_in - 1, 1), max(n_out - 1, 1)
    scratch = [
        pltpu.VMEM(features_in.shape, jnp.bfloat16),
        pltpu.VMEM(upstream.shape, jnp.bfloat16),
        pltpu.VMEM(kernel_taps.shape, jnp.bfloat16),
        pltpu.VMEM((1, out_chan), jnp.float32),
        dma((4,)),
        pltpu.VMEM((vols, planes * out_chan, cells), jnp.bfloat16),
        pltpu.VMEM((vols, cells // LANES, in_chan * planes, LANES), jnp.float32),
        pltpu.VMEM((vols, cells // LANES, out_chan * planes, LANES), jnp.float32),
        pltpu.VMEM((2, vols, in_chan, cells), jnp.bfloat16),
        pltpu.VMEM((2, vols, out_chan, cells), jnp.bfloat16),
        pltpu.VMEM((32 * half, LANES), jnp.float32),
        pltpu.VMEM((planes * out_chan, (planes + 2) * depth(in_chan)), jnp.bfloat16),
        pltpu.VMEM((planes * in_chan, (planes + 2) * depth(out_chan)), jnp.bfloat16),
        pltpu.VMEM((2, vols, in_chan, cells), jnp.bfloat16),
        pltpu.VMEM((2, vols, out_chan, cells), jnp.bfloat16),
        pltpu.VMEM((vols, (planes + 2) * depth(in_chan), cells), jnp.bfloat16),
        pltpu.VMEM((vols, (planes + 2) * depth(out_chan), cells), jnp.bfloat16),
        pltpu.VMEM((n_in, size_a, LANES), jnp.float32),
        pltpu.VMEM((n_in, size_b, LANES), jnp.float32),
        pltpu.VMEM((steps_in, size_a, LANES), jnp.float32),
        pltpu.VMEM((steps_in, size_b, LANES), jnp.float32),
        pltpu.VMEM((n_out, per, LANES), jnp.float32),
        pltpu.VMEM((steps_out, per, LANES), jnp.float32),
        pltpu.VMEM((n_in, n_out, per, LANES), jnp.bfloat16),
        pltpu.VMEM((n_in * size_a, LANES), jnp.float32),
        pltpu.VMEM((n_in * size_b, LANES), jnp.float32),
        dma((2, 2)),
        dma((2, 2)),
        dma((2, steps_in)),
        dma((2, steps_in)),
        dma((steps_out,)),
        dma((steps_out,)),
        dma((steps_out,)),
        dma((steps_out,)),
        dma((steps_in,)),
        dma((steps_in,)),
    ]
    held = [each for each in scratch if each.memory_space == pltpu.VMEM]
    grant = sum(math.prod(each.shape) * jnp.dtype(each.dtype).itemsize for each in held)
    results = pl.pallas_call(
        functools.partial(kernel, sizes, factor),
        out_shape=(
            jax.ShapeDtypeStruct(upstream.shape, jnp.bfloat16),
            jax.ShapeDtypeStruct(features_in.shape, jnp.bfloat16),
            jax.ShapeDtypeStruct(kernel_taps.shape, jnp.float32),
            jax.ShapeDtypeStruct((1, out_chan), jnp.float32),
        ),
        in_specs=[hbm] * 4,
        out_specs=(vmem,) * 4,
        scratch_shapes=scratch,
        compiler_params=pltpu.CompilerParams(
            collective_id=0, has_side_effects=True, vmem_limit_bytes=grant + 6 * 2**20
        ),
    )(
        pltpu.with_memory_space_constraint(features_in, pltpu.HBM),
        pltpu.with_memory_space_constraint(upstream, pltpu.HBM),
        pltpu.with_memory_space_constraint(kernel_taps, pltpu.HBM),
        pltpu.with_memory_space_constraint(channel_bias.reshape(1, out_chan), pltpu.HBM),
    )
    output, grad_input, weight_grad, bias_grad = pl.pallas_call(
        finish,
        out_shape=tuple(jax.ShapeDtypeStruct(each.shape, each.dtype) for each in results),
        in_specs=[vmem] * 4,
        out_specs=(hbm,) * 4,
        scratch_shapes=[dma((4,))],
        compiler_params=pltpu.CompilerParams(vmem_limit_bytes=4 * 2**20),
    )(*results)
    return (output, grad_input, weight_grad, bias_grad.reshape(out_chan))


def solution(mesh):
    n_dp, n_gz = mesh.shape["dp"], mesh.shape["gz"]
    inner_dp = max(d for d in range(1, n_dp + 1) if n_dp % d == 0 and d * d <= n_dp)
    sizes = (inner_dp, n_gz, inner_dp * n_gz, n_dp // inner_dp)
    in_specs = (P("dp", None, "gz", None), P(), P(), P("dp", None, "gz", None))
    out_specs = (P("dp", None, "gz", None), P("dp", None, "gz", None), P(), P())
    return jax.shard_map(
        functools.partial(on_device, sizes),
        mesh=mesh,
        in_specs=in_specs,
        out_specs=out_specs,
        check_vma=False,
    )
```

```python
import functools
import math

import jax
import jax.numpy as jnp
from jax import lax
from jax.experimental import pallas as pl
from jax.experimental.pallas import tpu as pltpu
from jax.sharding import PartitionSpec as P

NX = 64
NY = 8
MESH = pl.DeviceIdType.MESH
LANES = 128
ROWS = 16


def shifted(field):
    cells = field.shape[1]
    at = lax.broadcasted_iota(jnp.int32, field.shape, 1)
    col = at % NX
    zero = jnp.zeros_like(field)
    sides = (
        jnp.where(col == 0, zero, pltpu.roll(field, 1, 1)),
        field,
        jnp.where(col == NX - 1, zero, pltpu.roll(field, cells - 1, 1)),
    )
    found = [jnp.where(at < NX, zero, pltpu.roll(side, NX, 1)) for side in sides]
    found += list(sides)
    found += [jnp.where(at >= cells - NX, zero, pltpu.roll(side, cells - NX, 1)) for side in sides]
    return [each.astype(jnp.bfloat16) for each in found]


def fill(buf, vol, start, chan, piece, field):
    for tap, value in enumerate(shifted(field)):
        buf[vol, pl.ds(start + tap * chan + piece * ROWS, ROWS), :] = value


def depth(chan):
    return LANES * -(-9 * chan // LANES)


def kernel(
    sizes, factor, x_hbm, u_hbm, taps_hbm, bias_hbm, out_ref, gi_ref, wg_ref, bg_ref,
    x_ref, u_ref, taps_ref, bias_ref, load, grads, rows_x, rows_u, edge_x, edge_u, taps_rows, wf, wb,
    halo_x, halo_u, near_x, near_u, part_a, part_b, recv_a, recv_b, acc, recv_out, gath,
    sums_a, sums_b,
    halo_send, halo_recv, in_send, in_recv, out_send, out_recv,
    gout_send, gout_recv, gin_send, gin_recv,
):
    inner_dp, n_gz, n_in, n_out = sizes
    vols, in_chan, planes, cells = x_ref.shape
    out_chan = u_ref.shape[1]
    half = in_chan // 2
    dp, gz = lax.axis_index("dp"), lax.axis_index("gz")
    me_in = lax.rem(dp, inner_dp) * n_gz + gz
    me_out = lax.div(dp, inner_dp)

    @functools.cache
    def inner_peer(step):
        peer = lax.rem(me_in + step, n_in)
        return peer, {"dp": me_out * inner_dp + lax.div(peer, n_gz), "gz": lax.rem(peer, n_gz)}

    @functools.cache
    def outer_peer(step):
        peer = lax.rem(me_out + step, n_out)
        return peer, {"dp": peer * inner_dp + lax.rem(dp, inner_dp), "gz": gz}

    tiles = cells // LANES

    def piece_x(vol, z, piece):
        at = pl.ds(piece * planes + z, half, stride=2 * planes)
        return jnp.concatenate([rows_x[vol, tile, at, :] for tile in range(tiles)], axis=1)

    def piece_u(vol, z, piece):
        at = pl.ds(piece * ROWS * planes + z, ROWS, stride=planes)
        return jnp.concatenate([rows_u[vol, tile, at, :] for tile in range(tiles)], axis=1)

    def spread(rows, vol, ref, chan):
        for i in range(chan):
            value = ref[vol, i].astype(jnp.float32)
            for tile in range(tiles):
                at = slice(tile * LANES, (tile + 1) * LANES)
                rows[vol, tile, pl.ds(i * planes, planes), :] = value[:, at]

    def put(rows, vol, at, value):
        for tile in range(tiles):
            rows[vol, tile, at, :] = value[:, tile * LANES : (tile + 1) * LANES]

    def unite(rows, vol, ref, chan):
        for i in range(chan):
            at = pl.ds(i * planes, planes)
            value = jnp.concatenate([rows[vol, tile, at, :] for tile in range(tiles)], axis=1)
            ref[vol, i] = value.astype(jnp.bfloat16)

    moves = ((x_hbm, x_ref), (u_hbm, u_ref), (taps_hbm, taps_ref), (bias_hbm, bias_ref))
    loads = [
        pltpu.make_async_copy(source, target, load.at[at])
        for at, (source, target) in enumerate(moves)
    ]
    for copy in loads:
        copy.start()
    barrier = pltpu.get_barrier_semaphore()
    for step in range(1, n_in):
        pl.semaphore_signal(barrier, inc=1, device_id=inner_peer(step)[1], device_id_type=MESH)
    for step in range(1, n_out):
        pl.semaphore_signal(barrier, inc=1, device_id=outer_peer(step)[1], device_id_type=MESH)

    deep_x, deep_u = depth(in_chan), depth(out_chan)
    wb[...] = jnp.zeros_like(wb)
    wf[...] = jnp.zeros_like(wf)
    for vol in range(vols):
        for near, deep, chan in ((near_x, deep_x, in_chan), (near_u, deep_u, out_chan)):
            pad = deep - 9 * chan
            if pad:
                for slot in range(planes + 2):
                    at = pl.ds(slot * deep + 9 * chan, pad)
                    near[vol, at, :] = jnp.zeros((pad, cells), jnp.bfloat16)
    loads[0].wait()
    for vol in range(vols):
        spread(rows_x, vol, x_ref, in_chan)
        for side, z in ((0, planes - 1), (1, 0)):
            for piece in range(2):
                at = pl.ds(piece * half, half)
                edge_x[side, vol, at, :] = piece_x(vol, z, piece).astype(jnp.bfloat16)

    pl.semaphore_wait(barrier, n_in + n_out - 2)

    def halo_copies(side, which=(0, 1)):
        target = gz + 1 if side == 0 else gz - 1
        return [
            pltpu.make_async_remote_copy(
                src_ref=ref.at[side],
                dst_ref=halo.at[side],
                send_sem=halo_send.at[side, at],
                recv_sem=halo_recv.at[side, at],
                device_id={"gz": target},
                device_id_type=MESH,
            )
            for at, (ref, halo) in enumerate(((edge_x, halo_x), (edge_u, halo_u)))
            if at in which
        ]

    sends = (gz < n_gz - 1, gz > 0)
    gets = (gz > 0, gz < n_gz - 1)
    def send_halos(which):
        for side in range(2):

            @pl.when(sends[side])
            def _(side=side):
                halo_copies(side, (which,))[0].start()

    send_halos(0)
    loads[1].wait()
    for vol in range(vols):
        spread(rows_u, vol, u_ref, out_chan)
        for z in range(planes):
            for piece in range(out_chan // ROWS):
                value = piece_u(vol, z, piece).astype(jnp.bfloat16)
                grads[vol, pl.ds(z * out_chan + piece * ROWS, ROWS), :] = value
        for side, z in ((0, planes - 1), (1, 0)):
            edge_u[side, vol] = grads[vol, pl.ds(z * out_chan, out_chan), :]
    lanes = (((1,), (1,)), ((), ()))
    for vol in range(vols):
        for z in range(planes):
            for piece in range(2):
                fill(near_x, vol, (z + 1) * deep_x, in_chan, piece, piece_x(vol, z, piece))

    def product(vol, slot, at, wide):
        window = near_x[vol, pl.ds(slot * deep_x, 9 * in_chan), :]
        grad = grads[vol, pl.ds(at, wide), :]
        return lax.dot_general(window, grad, lanes, preferred_element_type=jnp.float32)

    def lane_tile(value, k):
        return value[:, k * LANES : (k + 1) * LANES]

    last = planes * out_chan - LANES
    even = [jnp.zeros((9 * in_chan, LANES), jnp.float32) for _ in range(3)]
    odd = [jnp.zeros((9 * in_chan, LANES), jnp.float32) for _ in range(3)]
    ones = jnp.ones((8, cells), jnp.bfloat16)
    bias_term = jnp.zeros((8, LANES), jnp.float32)
    for vol in range(vols):
        for slot in range(1, planes + 1):
            inside = product(vol, slot, 0, planes * out_chan)
            for tap in range(3):
                z = slot - tap
                if 0 <= z < planes:
                    kept = odd if z % 2 else even
                    kept[tap] += lane_tile(inside, z // 2)
        bias_all = lax.dot_general(
            ones, grads[vol], lanes, preferred_element_type=jnp.float32
        )
        for k in range(planes // 2):
            bias_term += lane_tile(bias_all, k)

    def packed(tap):
        first = even[tap].reshape(9, 2, half, LANES)
        second = odd[tap].reshape(9, 2, half, LANES)
        low = lax.broadcasted_iota(jnp.int32, (9, half, LANES), 2) < out_chan
        stay = jnp.where(low, first[:, 0], second[:, 1]).reshape(9 * half, LANES)
        move = jnp.where(low, first[:, 1], second[:, 0]).reshape(9 * half, LANES)
        return stay + pltpu.roll(move, out_chan, 1)

    def lay(part, pieces):
        rest = math.prod(part.shape[:2]) - sum(each.shape[0] for each in pieces)
        if rest:
            pieces = pieces + [jnp.zeros((rest, LANES), jnp.float32)]
        part[...] = jnp.concatenate(pieces, axis=0).reshape(part.shape)

    def in_copy(step, second):
        peer, device = inner_peer(step)
        return pltpu.make_async_remote_copy(
            src_ref=(part_b if second else part_a).at[peer],
            dst_ref=(recv_b if second else recv_a).at[step - 1],
            send_sem=in_send.at[second, step - 1],
            recv_sem=in_recv.at[second, step - 1],
            device_id=device,
            device_id_type=MESH,
        )

    bias_term += pltpu.roll(bias_term, out_chan, 1)
    lay(part_a, [packed(1), bias_term])
    for step in range(1, n_in):
        in_copy(step, 0).start()

    for side in range(2):

        @pl.when(gets[side])
        def _(side=side):
            halo_copies(side, (0,))[0].wait_recv()

        @pl.when(jnp.logical_not(gets[side]))
        def _(side=side):
            halo_x[side] = jnp.zeros(halo_x.shape[1:], halo_x.dtype)
            halo_u[side] = jnp.zeros(halo_u.shape[1:], halo_u.dtype)

    for vol in range(vols):
        for side, slot in ((0, 0), (1, planes + 1)):
            for piece in range(2):
                field = halo_x[side, vol, pl.ds(piece * half, half), :].astype(jnp.float32)
                fill(near_x, vol, slot * deep_x, in_chan, piece, field)
        even[0] += product(vol, 0, 0, LANES)
        odd[2] += product(vol, planes + 1, last, LANES)
    lay(part_b, [packed(0), packed(2)])
    for step in range(1, n_in):
        in_copy(step, 1).start()

    def out_copy(step):
        peer, device = outer_peer(step)
        return pltpu.make_async_remote_copy(
            src_ref=acc.at[peer],
            dst_ref=recv_out.at[step - 1],
            send_sem=out_send.at[step - 1],
            recv_sem=out_recv.at[step - 1],
            device_id=device,
            device_id_type=MESH,
        )

    def gather_out_copy(step):
        return pltpu.make_async_remote_copy(
            src_ref=gath.at[me_in, me_out],
            dst_ref=gath.at[me_in, me_out],
            send_sem=gout_send.at[step - 1],
            recv_sem=gout_recv.at[step - 1],
            device_id=outer_peer(step)[1],
            device_id_type=MESH,
        )

    def gather_in_copy(step):
        return pltpu.make_async_remote_copy(
            src_ref=gath.at[me_in],
            dst_ref=gath.at[me_in],
            send_sem=gin_send.at[step - 1],
            recv_sem=gin_recv.at[step - 1],
            device_id=inner_peer(step)[1],
            device_id_type=MESH,
        )

    loads[2].wait()
    loads[3].wait()
    stride = taps_rows.shape[0] // half
    for j in range(half):
        taps_rows[pl.ds(j * stride, 27), :] = taps_ref[:, pl.ds(j * LANES, LANES)].astype(jnp.float32)

    def tap_kernel(t):
        both = taps_rows[pl.ds(t, half, stride=stride), :]
        return jnp.concatenate([both[:, :out_chan], both[:, out_chan:]], axis=0)

    group = LANES // in_chan
    for a in range(3):
        for t in range(0, 9, group):
            some = [tap_kernel(9 * a + t + k) for k in range(min(group, 9 - t))]
            some = jnp.concatenate(some, axis=0).T.astype(jnp.bfloat16)
            for z in range(planes):
                at = pl.ds((z + a) * deep_x + t * in_chan, some.shape[1])
                wf[pl.ds(z * out_chan, out_chan), at] = some
    for a in range(3):
        for t in range(0, 9, 2):
            some = [tap_kernel(26 - 9 * a - t - k) for k in range(min(2, 9 - t))]
            some = jnp.concatenate(some, axis=1).astype(jnp.bfloat16)
            for z in range(planes):
                at = pl.ds((z + a) * deep_u + t * out_chan, some.shape[1])
                wb[pl.ds(z * in_chan, in_chan), at] = some

    for vol in range(vols):
        for z in range(planes):
            for piece in range(out_chan // ROWS):
                fill(near_u, vol, (z + 1) * deep_u, out_chan, piece, piece_u(vol, z, piece))

    rows = (((1,), (0,)), ((), ()))
    for step in range(1, n_in):
        in_copy(step, 0).wait_recv()
        in_copy(step, 1).wait_recv()
    total_a, total_b = part_a[me_in], part_b[me_in]
    for step in range(1, n_in):
        total_a += recv_a[step - 1]
        total_b += recv_b[step - 1]
    acc[...] = jnp.concatenate([total_a, total_b], axis=0).reshape(acc.shape)
    for step in range(1, n_out):
        out_copy(step).start()
    send_halos(1)

    bias = jnp.broadcast_to(bias_ref[...], (LANES, out_chan)).T
    bias = jnp.concatenate([bias] * (cells // LANES), axis=1)
    for vol in range(vols):
        value = lax.dot_general(wf[...], near_x[vol], rows, preferred_element_type=jnp.float32)
        for z in range(planes):
            plane = value[z * out_chan : (z + 1) * out_chan]
            put(rows_u, vol, pl.ds(z, out_chan, stride=planes), plane + bias)

    def backward(first):
        tile = min(2 * LANES, cells)
        for vol in range(vols):
            for at in range(0 if first else tile, tile if first else cells, tile):
                field = near_u[vol, :, pl.ds(at, tile)]
                value = lax.dot_general(wb[...], field, rows, preferred_element_type=jnp.float32)
                for z in range(planes):
                    for piece in range(2):
                        low = z * in_chan + piece * half
                        out = pl.ds(piece * planes + z, half, stride=2 * planes)
                        for k in range(tile // LANES):
                            part_k = value[low : low + half, k * LANES : (k + 1) * LANES]
                            rows_x[vol, at // LANES + k, out, :] = part_k

    for step in range(1, n_out):
        out_copy(step).wait_recv()
    total = acc[me_out]
    for step in range(1, n_out):
        total += recv_out[step - 1]
    gath[me_in, me_out] = (total * factor).astype(jnp.bfloat16)
    for step in range(1, n_out):
        gather_out_copy(step).start()
    for side in range(2):

        @pl.when(gets[side])
        def _(side=side):
            halo_copies(side, (1,))[0].wait_recv()

    for vol in range(vols):
        for side, slot in ((0, 0), (1, planes + 1)):
            for piece in range(out_chan // ROWS):
                field = halo_u[side, vol, pl.ds(piece * ROWS, ROWS), :].astype(jnp.float32)
                fill(near_u, vol, slot * deep_u, out_chan, piece, field)
    backward(True)
    for step in range(1, n_out):
        gather_out_copy(step).wait_recv()
    for step in range(1, n_in):
        gather_in_copy(step).start()
    for vol in range(vols):
        unite(rows_u, vol, out_ref, out_chan)
    backward(False)
    for vol in range(vols):
        unite(rows_x, vol, gi_ref, in_chan)
    for step in range(1, n_in):
        gather_in_copy(step).wait_recv()
    size_a, size_b = part_a.shape[1], part_b.shape[1]
    for peer in range(n_in):
        value = gath[peer].astype(jnp.float32).reshape(size_a + size_b, LANES)
        sums_a[pl.ds(peer * size_a, size_a), :] = value[:size_a]
        sums_b[pl.ds(peer * size_b, size_b), :] = value[size_a:]
    for j in range(half):
        value = [
            sums_b[pl.ds(j, 9, stride=half), :],
            sums_a[pl.ds(j, 9, stride=half), :],
            sums_b[pl.ds(9 * half + j, 9, stride=half), :],
        ]
        wg_ref[:, pl.ds(j * LANES, LANES)] = jnp.concatenate(value, axis=0)
    bg_ref[...] = sums_a[pl.ds(9 * half, 1), :out_chan]

    for side in range(2):

        @pl.when(sends[side])
        def _(side=side):
            for copy in halo_copies(side):
                copy.wait_send()

    for step in range(1, n_in):
        in_copy(step, 0).wait_send()
        in_copy(step, 1).wait_send()
        gather_in_copy(step).wait_send()
    for step in range(1, n_out):
        out_copy(step).wait_send()
        gather_out_copy(step).wait_send()


def finish(*refs):
    sem = refs[8]
    copies = [pltpu.make_async_copy(refs[k], refs[4 + k], sem.at[k]) for k in range(4)]
    for copy in copies:
        copy.start()
    for copy in copies:
        copy.wait()


def on_device(sizes, features_in, kernel_taps, channel_bias, upstream):
    inner_dp, n_gz, n_in, n_out = sizes
    vols, in_chan, planes, cells = features_in.shape
    out_chan = upstream.shape[1]
    half = in_chan // 2
    cells_all = vols * inner_dp * n_out * planes * n_gz * cells
    factor = 1.0 / math.sqrt(cells_all)
    size_a = 8 * -(-(9 * half + 8) // (8 * n_in))
    size_b = 8 * -(-(18 * half) // (8 * n_in))
    per = ROWS * -(-(size_a + size_b) // (ROWS * n_out))
    size_b = n_out * per - size_a
    vmem = pl.BlockSpec(memory_space=pltpu.VMEM)
    hbm = pl.BlockSpec(memory_space=pltpu.HBM)
    dma = pltpu.SemaphoreType.DMA
    steps_in, steps_out = max(n_in - 1, 1), max(n_out - 1, 1)
    scratch = [
        pltpu.VMEM(features_in.shape, jnp.bfloat16),
        pltpu.VMEM(upstream.shape, jnp.bfloat16),
        pltpu.VMEM(kernel_taps.shape, jnp.bfloat16),
        pltpu.VMEM((1, out_chan), jnp.float32),
        dma((4,)),
        pltpu.VMEM((vols, planes * out_chan, cells), jnp.bfloat16),
        pltpu.VMEM((vols, cells // LANES, in_chan * planes, LANES), jnp.float32),
        pltpu.VMEM((vols, cells // LANES, out_chan * planes, LANES), jnp.float32),
        pltpu.VMEM((2, vols, in_chan, cells), jnp.bfloat16),
        pltpu.VMEM((2, vols, out_chan, cells), jnp.bfloat16),
        pltpu.VMEM((32 * half, LANES), jnp.float32),
        pltpu.VMEM((planes * out_chan, (planes + 2) * depth(in_chan)), jnp.bfloat16),
        pltpu.VMEM((planes * in_chan, (planes + 2) * depth(out_chan)), jnp.bfloat16),
        pltpu.VMEM((2, vols, in_chan, cells), jnp.bfloat16),
        pltpu.VMEM((2, vols, out_chan, cells), jnp.bfloat16),
        pltpu.VMEM((vols, (planes + 2) * depth(in_chan), cells), jnp.bfloat16),
        pltpu.VMEM((vols, (planes + 2) * depth(out_chan), cells), jnp.bfloat16),
        pltpu.VMEM((n_in, size_a, LANES), jnp.float32),
        pltpu.VMEM((n_in, size_b, LANES), jnp.float32),
        pltpu.VMEM((steps_in, size_a, LANES), jnp.float32),
        pltpu.VMEM((steps_in, size_b, LANES), jnp.float32),
        pltpu.VMEM((n_out, per, LANES), jnp.float32),
        pltpu.VMEM((steps_out, per, LANES), jnp.float32),
        pltpu.VMEM((n_in, n_out, per, LANES), jnp.bfloat16),
        pltpu.VMEM((n_in * size_a, LANES), jnp.float32),
        pltpu.VMEM((n_in * size_b, LANES), jnp.float32),
        dma((2, 2)),
        dma((2, 2)),
        dma((2, steps_in)),
        dma((2, steps_in)),
        dma((steps_out,)),
        dma((steps_out,)),
        dma((steps_out,)),
        dma((steps_out,)),
        dma((steps_in,)),
        dma((steps_in,)),
    ]
    held = [each for each in scratch if each.memory_space == pltpu.VMEM]
    grant = sum(math.prod(each.shape) * jnp.dtype(each.dtype).itemsize for each in held)
    results = pl.pallas_call(
        functools.partial(kernel, sizes, factor),
        out_shape=(
            jax.ShapeDtypeStruct(upstream.shape, jnp.bfloat16),
            jax.ShapeDtypeStruct(features_in.shape, jnp.bfloat16),
            jax.ShapeDtypeStruct(kernel_taps.shape, jnp.float32),
            jax.ShapeDtypeStruct((1, out_chan), jnp.float32),
        ),
        in_specs=[hbm] * 4,
        out_specs=(vmem,) * 4,
        scratch_shapes=scratch,
        compiler_params=pltpu.CompilerParams(
            collective_id=0, has_side_effects=True, vmem_limit_bytes=grant + 6 * 2**20
        ),
    )(
        pltpu.with_memory_space_constraint(features_in, pltpu.HBM),
        pltpu.with_memory_space_constraint(upstream, pltpu.HBM),
        pltpu.with_memory_space_constraint(kernel_taps, pltpu.HBM),
        pltpu.with_memory_space_constraint(channel_bias.reshape(1, out_chan), pltpu.HBM),
    )
    output, grad_input, weight_grad, bias_grad = pl.pallas_call(
        finish,
        out_shape=tuple(jax.ShapeDtypeStruct(each.shape, each.dtype) for each in results),
        in_specs=[vmem] * 4,
        out_specs=(hbm,) * 4,
        scratch_shapes=[dma((4,))],
        compiler_params=pltpu.CompilerParams(vmem_limit_bytes=4 * 2**20),
    )(*results)
    return (output, grad_input, weight_grad, bias_grad.reshape(out_chan))


def solution(mesh):
    n_dp, n_gz = mesh.shape["dp"], mesh.shape["gz"]
    inner_dp = max(d for d in range(1, n_dp + 1) if n_dp % d == 0 and d * d <= n_dp)
    sizes = (inner_dp, n_gz, inner_dp * n_gz, n_dp // inner_dp)
    in_specs = (P("dp", None, "gz", None), P(), P(), P("dp", None, "gz", None))
    out_specs = (P("dp", None, "gz", None), P("dp", None, "gz", None), P(), P())
    return jax.shard_map(
        functools.partial(on_device, sizes),
        mesh=mesh,
        in_specs=in_specs,
        out_specs=out_specs,
        check_vma=False,
    )
```
